32 devices in a mesh: ia: 4 (over y, x), ja: 8 (over z, core).
Axes of the slice: x: 2, y: 2, z: 4, core: 2. Of those that a mesh axis runs over, the one named last changes fastest.
Arguments:
- tensor: float32 [8, 8192, 8192], P(None, 'ia', 'ja'), may hold values from -6 to 6
- b_init: float32 [8192, 64], P('ja'), may hold values from -0.0625 to 0.0625
- c_init: float32 [8, 64], replicated, may hold values from -6 to 6
Outputs:
- factor_a: float32 [8192, 64], P(('ia', 'ja'))
- factor_b: float32 [8192, 64], P('ja')
- factor_c: float32 [8, 64], replicated
The draws below stay inside these ranges and needn't reach their ends.
All inputs are finite; a program needn't handle non-finite values.
Results may differ from the reference program's by a relative error of at most 0.0003.
Values sent between devices are 32-bit elements; how exact they have to be, the bound alone decides.
No kernel may reach another device: no remote copies, remote signals or barrier semaphores. Data moves between devices by JAX's collectives and lax.ppermute only.
A program may use at most 128 MiB of HBM per device.

```python
import jax
import jax.numpy as jnp
from jax import lax

I = 8192
J = 8192
K = 8
R = 64
SWEEPS = 4


def steps_of(own_key, extent, shards, least, top_value):
    def one(position, blocks):
        heights = jax.random.uniform(jax.random.fold_in(jax.random.fold_in(own_key, 6), position), (blocks,), jnp.float32, least / len(shards), top_value / len(shards))
        return jnp.repeat(jnp.exp(heights), extent[position] // blocks).reshape((-1,) + (1,) * (len(extent) - position - 1))

    level = one(*shards[0])
    for cut in shards[1:]:
        level = level * one(*cut)
    return level


def centred(key, dims, deviation, limit, pieces=(), dtype=jnp.bfloat16):
    values = deviation * jax.random.normal(key, dims, jnp.float32)
    if pieces:
        values = values * steps_of(key, dims, pieces, -0.22, 0.18)
    return jnp.clip(values, -limit, limit).astype(dtype)


def setup_inputs(seed: int = 0) -> dict:
    key_list = jax.random.split(jax.random.key(seed), 4)
    tensor = centred(key_list[0], (K, I, J), 1.0, 6.0, ((1, 4), (2, 8)), jnp.float32)
    b_init = centred(key_list[1], (J, R), J ** -0.5, 0.0625, ((0, 8),), jnp.float32)
    c_init = centred(key_list[2], (K, R), 1.0, 6.0, (), jnp.float32)
    return dict(tensor=tensor, b_init=b_init, c_init=c_init)


HIGH = lax.Precision.HIGHEST

def gram_of(factor):
    return jnp.dot(factor.T.astype(jnp.float32), factor.astype(jnp.float32), precision=HIGH, preferred_element_type=jnp.float32)

def solve_rows(products, normal):
    lower = jnp.linalg.cholesky(normal)
    return jax.scipy.linalg.cho_solve((lower, True), products.T).T

def unit_columns(factor, raw):
    norms = jnp.sqrt(jnp.diagonal(raw) + 1e-06)
    return (factor / norms[None, :], raw / (norms[:, None] * norms[None, :]))

def reference(tensor, b_init, c_init):
    factor_b = b_init
    factor_c = c_init
    gram_b = gram_of(factor_b)
    gram_c = gram_of(factor_c)
    factor_a = None
    for sweep in range(SWEEPS):
        partial_value = jnp.einsum('kij,jr->kir', tensor, factor_b, precision=HIGH)
        mode_one = jnp.einsum('kir,kr->ir', partial_value, factor_c, precision=HIGH)
        factor_a = solve_rows(mode_one, gram_b * gram_c)
        factor_a, gram_a = unit_columns(factor_a, gram_of(factor_a))
        partial_value = jnp.einsum('kij,ir->kjr', tensor, factor_a, precision=HIGH)
        mode_two = jnp.einsum('kjr,kr->jr', partial_value, factor_c, precision=HIGH)
        factor_b = solve_rows(mode_two, gram_a * gram_c)
        factor_b, gram_b = unit_columns(factor_b, gram_of(factor_b))
        partial_value = jnp.einsum('kij,jr->kir', tensor, factor_b, precision=HIGH)
        mode_three = jnp.einsum('kir,ir->kr', partial_value, factor_a, precision=HIGH)
        factor_c = solve_rows(mode_three, gram_a * gram_b)
        gram_c = gram_of(factor_c)
    return (factor_a, factor_b, factor_c)
```

```python
import functools

import jax
import jax.numpy as jnp
from jax import lax
from jax.experimental import pallas as pl
from jax.experimental.pallas import tpu as pltpu
from jax.sharding import PartitionSpec as P

SWEEPS = 4
EPS = 1e-6
HIGH = lax.Precision.HIGHEST
F32 = jnp.float32
BF16 = jnp.bfloat16
VMEM = pl.BlockSpec(memory_space=pltpu.VMEM)
SMEM = pl.BlockSpec(memory_space=pltpu.SMEM)
MIB = 1 << 20


def params(mib):
    return pltpu.CompilerParams(vmem_limit_bytes=mib * MIB)


def cost(flops, nbytes):
    return pl.CostEstimate(flops=int(flops), bytes_accessed=int(nbytes), transcendentals=0)


def shape(*dims, dtype=F32):
    return jax.ShapeDtypeStruct(dims, dtype)


def dot(a, b, dims=((1,), (0,))):
    return lax.dot_general(a, b, (dims, ((), ())), precision=HIGH, preferred_element_type=F32)


def dot16(a, b):
    return jnp.dot(a, b, preferred_element_type=F32)


def split(x):
    hi = x.astype(BF16)
    return hi, (x - hi.astype(F32)).astype(BF16)


def iota(rows, cols, dim):
    return lax.broadcasted_iota(jnp.int32, (rows, cols), dim)


def eye(n):
    return (iota(n, n, 0) == iota(n, n, 1)).astype(F32)


def column_norms(raw):
    diagonal = raw * eye(raw.shape[0])
    row = jnp.sqrt(jnp.sum(diagonal, axis=0, keepdims=True) + EPS)
    col = jnp.sqrt(jnp.sum(diagonal, axis=1, keepdims=True) + EPS)
    return row, col


def inverse(g):
    n = g.shape[0]
    m = jnp.concatenate([g, eye(n)], axis=1)
    rows = iota(n, 2 * n, 0)
    for k in range(n):
        pivot = m[k : k + 1, :] / m[k : k + 1, k : k + 1]
        m = jnp.where(rows == k, pivot, m - m[:, k : k + 1] * pivot)
    return m[:, n:]


def block_diagonal(g):
    zero = jnp.zeros_like(g)
    return jnp.concatenate(
        [jnp.concatenate([g, zero], axis=1), jnp.concatenate([zero, g], axis=1)], axis=0
    )


def wide(x):
    return jnp.concatenate([x, x], axis=1)


def start_kernel(b_ref, c_ref, bt_ref, gb_ref, cs_ref, c_out, gc_ref):
    b = b_ref[...]
    bt_ref[...] = b.T
    gb_ref[...] = wide(dot(b, b, ((0,), (0,))))
    c = c_ref[...]
    c_out[...] = wide(c)
    cs_ref[...] = wide(c)
    gc_ref[...] = dot(c, c, ((0,), (0,)))


def sum_tree(parts):
    while len(parts) > 1:
        parts = [parts[i] + parts[i + 1] for i in range(0, len(parts), 2)]
    return parts[0]


def gram_b_start_kernel(*refs):
    grams, (gc_ref, gb_out, inv_out) = refs[:-3], refs[-3:]
    gram_b = sum_tree([g[...] for g in grams])[:, :64]
    gb_out[...] = gram_b
    inv_out[...] = block_diagonal(inverse(gram_b * gc_ref[...]))


def gram_b_kernel(*refs):
    grams, (ga_ref, na_ref, gb_out, nb_out, nbt_out, scale_out, inv_out) = refs[:-7], refs[-7:]
    raw = sum_tree([g[...] for g in grams])[:, :64]
    row, col = column_norms(raw)
    gram_b = raw / (row * col)
    gb_out[...] = gram_b
    nb_out[...] = row
    nbt_out[...] = col
    scale_out[...] = na_ref[...] * row
    inv_out[...] = inverse(gram_b * ga_ref[...])


def inverse_kernel(x_ref, y_ref, out_ref):
    out_ref[...] = block_diagonal(inverse(x_ref[...] * y_ref[...]))


def new_c(threes, scale_ref, inv_ref):
    total = sum_tree([t[...] for t in threes])
    return dot((total[:, :64] + total[:, 64:]) / scale_ref[...], inv_ref[...])


def final_c_kernel(*refs):
    threes, (scale_ref, inv_ref, c_out) = refs[:-3], refs[-3:]
    c_out[...] = new_c(threes, scale_ref, inv_ref)


def contract(core_ref, stored_ref, scaled, keep_ref, send_ref):
    depth, rows, _ = stored_ref.shape
    part = rows // 2
    chunk = min(64, part)
    core = core_ref[0]
    for out, which in ((keep_ref, core), (send_ref, 1 - core)):

        @pl.loop(0, part // chunk)
        def _(i):
            at = pl.multiple_of(which * part + i * chunk, chunk)
            total = stored_ref[0, pl.ds(at, chunk), :] * scaled[0:1, :]
            for k in range(1, depth):
                total = total + stored_ref[k, pl.ds(at, chunk), :] * scaled[k : k + 1, :]
            out[pl.ds(pl.multiple_of(i * chunk, chunk), chunk), :] = total


def contract_start_kernel(core_ref, stored_ref, cs_ref, keep_ref, send_ref):
    contract(core_ref, stored_ref, cs_ref[...], keep_ref, send_ref)


def contract_kernel(*refs):
    core_ref, stored_ref = refs[:2]
    threes = refs[2:-7]
    scale_ref, inv_ref, nb_ref, c_out, gc_out, keep_ref, send_ref = refs[-7:]
    c = new_c(threes, scale_ref, inv_ref)
    c_out[...] = wide(c)
    gc_out[...] = dot(c, c, ((0,), (0,)))
    contract(core_ref, stored_ref, wide(c / nb_ref[...]), keep_ref, send_ref)


def spread_kernel(z_ref, keep_ref, recv_ref, own_ref, *send_refs):
    rows = own_ref.shape[0]
    for d, out in enumerate((own_ref,) + send_refs):
        at = pl.multiple_of((z_ref[0] ^ d) * rows, rows)
        out[...] = keep_ref[pl.ds(at, rows), :] + recv_ref[pl.ds(at, rows), :]


def gather_kernel(z_ref, *refs):
    parts, out = refs[:-1], refs[-1]
    rows = parts[0].shape[0]
    for d, part in enumerate(parts):
        at = pl.multiple_of((z_ref[0] ^ d) * rows, rows)
        out[pl.ds(at, rows), :] = part[...]


def pass_a_kernel(core_ref, t_ref, half_ref, other_ref, inv_ref, c_ref,
                  a_out, first_out, second_out, at_ref, w_ref, acc_ref, low_ref, gram_ref):
    k, i = pl.program_id(0), pl.program_id(1)
    last_k, last_i = pl.num_programs(0) - 1, pl.num_programs(1) - 1
    rows = a_out.shape[0]
    part = rows // 2
    blocks, _, width = w_ref.shape

    @pl.when((k == 0) & (i == 0))
    def _():
        core = core_ref[0]
        inv = inv_ref[...]
        a_out[pl.ds(pl.multiple_of(core * part, part), part), :] = dot(half_ref[...], inv)
        a_out[pl.ds(pl.multiple_of((1 - core) * part, part), part), :] = dot(other_ref[...], inv)
        a = a_out[...]
        gram = dot(a, a, ((0,), (0,)))
        gram_ref[...] = gram[:64, :64] + gram[64:, 64:]
        at_ref[...] = a.T
        acc_ref[...] = jnp.zeros_like(acc_ref)
        low_ref[...] = jnp.zeros_like(low_ref)

    @pl.when(i == 0)
    def _():
        picked = jnp.where(iota(*c_ref.shape, 0) == k, c_ref[...], 0.0)
        row = jnp.sum(picked, axis=0, keepdims=True)[:, :64]
        col = jnp.sum(eye(64) * row, axis=1, keepdims=True)
        for b in range(blocks):
            half, q = divmod(b * width, rows)
            w = at_ref[64 * half : 64 * half + 64, q : q + width] * col
            hi, lo = split(w)
            w_ref[b, :64, :] = hi
            w_ref[b, 64:, :] = lo

    t = t_ref[0]
    hi, lo = split(t)
    acc_ref[...] += dot16(w_ref[i], hi)
    low_ref[...] += dot16(w_ref[i, :64, :], lo)

    @pl.when((k == last_k) & (i == last_i))
    def _():
        total = acc_ref[:64, :] + (acc_ref[64:, :] + low_ref[...])
        columns = total.shape[1]
        first_out[:, :columns] = total[:32]
        second_out[:, :columns] = total[32:]
        gram = wide(gram_ref[...])
        first_out[:, columns:] = gram[:32]
        second_out[:, columns:] = gram[32:]


def solve_b_kernel(a0_ref, a1_ref, b0_ref, b1_ref, gc_ref, bt_out, gb_out, ga_out, na_out, nac_out):
    total = jnp.concatenate([a0_ref[...] + a1_ref[...], b0_ref[...] + b1_ref[...]], axis=0)
    columns = bt_out.shape[1]
    raw = total[:, columns : columns + 64]
    row, col = column_norms(raw)
    gram_a = raw / (row * col)
    inv = inverse(gram_a * gc_ref[...])
    bt = dot(inv, total[:, :columns] / col)
    bt_out[...] = bt
    gb_out[...] = wide(dot(bt, bt, ((1,), (1,))))
    ga_out[...] = gram_a
    na_out[...] = row
    nac_out[...] = wide(row)


def pass_b_kernel(with_three, with_stored, *refs):
    t_ref, bt_ref = refs[:2]
    refs = refs[2:]
    a_ref = stored_ref = three_ref = None
    if with_three:
        a_ref, refs = refs[0], refs[1:]
    if with_stored:
        stored_ref, refs = refs[0], refs[1:]
    if with_three:
        three_ref, refs = refs[0], refs[1:]
    (w_ref,) = refs
    k, q = pl.program_id(0), pl.program_id(1)

    @pl.when((k == 0) & (q == 0))
    def _():
        hi, lo = split(bt_ref[...])
        b = jnp.concatenate([hi.astype(F32), lo.astype(F32)], axis=0).T.astype(F32)
        zero = jnp.zeros((b.shape[0], 64), F32)
        b_hi, b_lo = b[:, :64], b[:, 64:]
        w_ref[0] = jnp.concatenate([b_hi, zero, b_lo, zero], axis=1).astype(BF16)
        w_ref[1] = jnp.concatenate([zero, b_hi, zero, b_lo], axis=1).astype(BF16)
        if with_three:
            three_ref[...] = jnp.zeros_like(three_ref)

    total = None
    for half in range(2):
        hi, lo = split(t_ref[0, half])
        both = dot16(hi, w_ref[half])
        part = both[:, :128] + (both[:, 128:] + dot16(lo, w_ref[half, :, :128]))
        total = part if total is None else total + part
    if with_stored:
        stored_ref[0] = total
    if with_three:
        sums = jnp.sum(total * a_ref[...], axis=0, keepdims=True)
        three_ref[...] += jnp.where(iota(*three_ref.shape, 0) == k, sums, 0.0)


def pass_a(core, tensor, half, other, inv, c_wide):
    depth, rows, columns = tensor.shape
    block = min(512, rows // 2)
    return pl.pallas_call(
        pass_a_kernel,
        grid=(depth, rows // block),
        in_specs=[
            SMEM,
            pl.BlockSpec((1, block, columns), lambda k, i: (k, i, 0)),
            VMEM, VMEM, VMEM, VMEM,
        ],
        out_specs=[VMEM, VMEM, VMEM],
        out_shape=[
            shape(rows // 2, 128), shape(32, columns + 128), shape(32, columns + 128),
        ],
        scratch_shapes=[
            pltpu.VMEM((128, rows // 2), F32),
            pltpu.VMEM((rows // block, 128, block), BF16),
            pltpu.VMEM((128, columns), F32),
            pltpu.VMEM((64, columns), F32),
            pltpu.VMEM((64, 64), F32),
        ],
        compiler_params=params(40),
        cost_estimate=cost(4 * tensor.size * 128, 4 * tensor.size),
        name="pass_a",
    )(core, tensor, half, other, inv, c_wide)


def pass_b(tensor, bt, a, with_stored):
    depth, rows, columns = tensor.shape
    half = rows // 2
    block = min(256, half)
    with_three = a is not None
    in_specs = [
        pl.BlockSpec((1, 2, block, columns), lambda k, q: (k, 0, q, 0)),
        VMEM,
    ]
    operands = [tensor.reshape(depth, 2, half, columns), bt]
    out_specs, out_shape = [], []
    if with_three:
        in_specs.append(pl.BlockSpec((block, 128), lambda k, q: (q, 0)))
        operands.append(a)
    if with_stored:
        out_specs.append(pl.BlockSpec((1, block, 128), lambda k, q: (k, q, 0)))
        out_shape.append(shape(depth, half, 128))
    if with_three:
        out_specs.append(VMEM)
        out_shape.append(shape(depth, 128))
    return pl.pallas_call(
        functools.partial(pass_b_kernel, with_three, with_stored),
        grid=(depth, half // block),
        in_specs=in_specs,
        out_specs=out_specs,
        out_shape=out_shape,
        scratch_shapes=[pltpu.VMEM((2, columns, 256), BF16)],
        compiler_params=params(40),
        cost_estimate=cost(4 * tensor.size * 128, 4 * tensor.size),
        name="pass_b",
    )(*operands)


def small(kernel, outs, *operands, smem=0, name=None, flops=200000, nbytes=200000):
    return pl.pallas_call(
        kernel,
        in_specs=[SMEM] * smem + [VMEM] * (len(operands) - smem),
        out_specs=[VMEM] * len(outs),
        out_shape=outs,
        compiler_params=params(24),
        cost_estimate=cost(flops, nbytes),
        name=name,
    )(*operands)


def across(x, axis, mask):
    n = lax.axis_size(axis)
    return lax.ppermute(x, axis, [(i, i ^ mask) for i in range(n)])


def body(tensor, b_init, c_init):
    depth, rows, columns = tensor.shape
    half = rows // 2
    n_ia, n_ja = lax.axis_size("ia"), lax.axis_size("ja")
    n_z = n_ja // 2
    ja = lax.axis_index("ja")
    core, z = (ja % 2).reshape(1), (ja // 2).reshape(1)
    piece = half // 2 // n_z
    bits = [1 << b for b in range(n_ia.bit_length() - 1)]

    def everyone(x, axis):
        return [x] + [across(x, axis, d) for d in range(1, lax.axis_size(axis))]

    def sum_over_ja(keep, send):
        recv = across(send, "ja", 1)
        own, *sends = small(
            spread_kernel, [shape(piece, 128)] * n_z, z, keep, recv, smem=1, name="spread"
        )
        own = sum_tree([own] + [across(s, "ja", 2 * d) for d, s in enumerate(sends, 1)])
        parts = [own] + [across(own, "ja", 2 * d) for d in range(1, n_z)]
        (mine,) = small(gather_kernel, [shape(half // 2, 128)], z, *parts, smem=1, name="gather")
        return mine, across(mine, "ja", 1)

    def sum_over_ia(first, second):
        order = bits + bits
        for step in range(len(bits) - 1):
            first = first + across(first, "ia", order[step])
            second = second + across(second, "ia", order[step + 1])
        step = len(bits) - 1
        return first, across(first, "ia", order[step]), second, across(second, "ia", order[step + 1])

    bt, gram, scaled, c_wide, gram_c = small(
        start_kernel,
        [shape(64, columns), shape(64, 128), shape(depth, 128), shape(depth, 128), shape(64, 64)],
        b_init, c_init, name="start",
    )
    grams = everyone(gram, "ja")
    (stored,) = pass_b(tensor, bt, None, True)
    keep, send = small(
        contract_start_kernel, [shape(half // 2, 128)] * 2, core, stored, scaled,
        smem=1, name="contract", flops=stored.size * 2, nbytes=stored.size * 4,
    )
    gram_b, inv = small(
        gram_b_start_kernel, [shape(64, 64), shape(128, 128)], *grams, gram_c, name="gram_b",
    )
    for sweep in range(SWEEPS):
        mine, other = sum_over_ja(keep, send)
        a, first, second = pass_a(core, tensor, mine, other, inv, c_wide)
        bt, gram, gram_a, norm_a, norm_a_wide = small(
            solve_b_kernel,
            [shape(64, columns), shape(64, 128), shape(64, 64), shape(1, 64), shape(1, 128)],
            *sum_over_ia(first, second), gram_c, name="solve_b",
        )
        grams = everyone(gram, "ja")
        last = sweep == SWEEPS - 1
        *stored, three = pass_b(tensor, bt, a, not last)
        gram_b, norm_b, norm_b_col, scale, inv = small(
            gram_b_kernel,
            [shape(64, 64), shape(1, 64), shape(64, 1), shape(1, 64), shape(64, 64)],
            *grams, gram_a, norm_a, name="gram_b",
        )
        three = sum_tree(everyone(three, "ja"))
        threes = everyone(three, "ia")
        if last:
            (factor_c,) = small(final_c_kernel, [shape(depth, 64)], *threes, scale, inv, name="final_c")
            break
        c_wide, gram_c, keep, send = small(
            contract_kernel,
            [shape(depth, 128), shape(64, 64), shape(half // 2, 128), shape(half // 2, 128)],
            core, *stored, *threes, scale, inv, norm_b,
            smem=1, name="contract", flops=stored[0].size * 2, nbytes=stored[0].size * 4,
        )
        (inv,) = small(inverse_kernel, [shape(128, 128)], gram_b, gram_c, name="inverse")
    factor_b = (bt / norm_b_col).T
    share = rows // n_ja
    at = ja * share
    mine = lax.dynamic_slice_in_dim(a / norm_a_wide, at % half, share, 0)
    factor_a = jnp.where(at < half, mine[:, :64], mine[:, 64:])
    return factor_a, factor_b, factor_c


def solution(mesh):
    in_specs = (P(None, "ia", "ja"), P("ja", None), P())
    out_specs = (P(("ia", "ja"), None), P("ja", None), P())
    return jax.shard_map(body, mesh=mesh, in_specs=in_specs, out_specs=out_specs, check_vma=False)
```

```python
import functools

import jax
import jax.numpy as jnp
from jax import lax
from jax.experimental import pallas as pl
from jax.experimental.pallas import tpu as pltpu
from jax.sharding import PartitionSpec as P

SWEEPS = 4
EPS = 1e-6
HIGH = lax.Precision.HIGHEST
F32 = jnp.float32
BF16 = jnp.bfloat16
F8 = jnp.float8_e4m3fn
TOP = 224.0
TINY = 1e-30
VMEM = pl.BlockSpec(memory_space=pltpu.VMEM)
MIB = 1 << 20


def params(mib):
    return pltpu.CompilerParams(vmem_limit_bytes=mib * MIB)


def cost(flops, nbytes):
    return pl.CostEstimate(flops=int(flops), bytes_accessed=int(nbytes), transcendentals=0)


def shape(*dims, dtype=F32):
    return jax.ShapeDtypeStruct(dims, dtype)


def dot(a, b, dims=((1,), (0,))):
    return lax.dot_general(a, b, (dims, ((), ())), precision=HIGH, preferred_element_type=F32)


def dot16(a, b):
    return jnp.dot(a, b, preferred_element_type=F32)


def split(x):
    hi = x.astype(BF16)
    return hi, (x - hi.astype(F32)).astype(BF16)


def iota(rows, cols, dim):
    return lax.broadcasted_iota(jnp.int32, (rows, cols), dim)


def eye(n):
    return (iota(n, n, 0) == iota(n, n, 1)).astype(F32)


def column_norms(raw):
    diagonal = raw * eye(raw.shape[0])
    row = jnp.sqrt(jnp.sum(diagonal, axis=0, keepdims=True) + EPS)
    col = jnp.sqrt(jnp.sum(diagonal, axis=1, keepdims=True) + EPS)
    return row, col


def eliminate(g):
    n = g.shape[0]
    m = jnp.concatenate([g, eye(n)], axis=1)
    rows = iota(n, 2 * n, 0)
    for k in range(n):
        pivot = m[k : k + 1, :] / m[k : k + 1, k : k + 1]
        m = jnp.where(rows == k, pivot, m - m[:, k : k + 1] * pivot)
    return m[:, n:]


def invert_into(out_ref, g):
    n = g.shape[0]
    one = eye(n)
    diagonal = g * one
    row = lax.rsqrt(jnp.sum(diagonal, axis=0, keepdims=True))
    col = lax.rsqrt(jnp.sum(diagonal, axis=1, keepdims=True))
    power = one - g * (row * col)
    close = jnp.sum(power * power) <= 0.25

    @pl.when(close)
    def _():
        e = power
        total = one + e
        for _ in range(4):
            e = dot(e, e)
            total = total + dot(total, e)
        out_ref[...] = total * (row * col)

    @pl.when(jnp.logical_not(close))
    def _():
        out_ref[...] = eliminate(g)


def block_diagonal(g):
    zero = jnp.zeros_like(g)
    return jnp.concatenate(
        [jnp.concatenate([g, zero], axis=1), jnp.concatenate([zero, g], axis=1)], axis=0
    )


def wide(x):
    return jnp.concatenate([x, x], axis=1)


def row_of(col):
    return jnp.sum(eye(col.shape[0]) * col, axis=0, keepdims=True)


def col_of(row):
    return jnp.sum(eye(row.shape[1]) * row, axis=1, keepdims=True)


def split8(x, unit):
    x = x / unit
    hi = x.astype(F8).astype(F32)
    return hi, ((x - hi) * 16.0).astype(F8).astype(F32)


def start_kernel(share, b_ref, c_ref, bt_ref, gb_ref, c_out, gc_ref):
    b = b_ref[...]
    bt_ref[...] = b.T
    gb_ref[...] = wide(dot(b, b, ((0,), (0,))))
    c = c_ref[...]
    c_out[...] = wide(c)
    gc_ref[...] = dot(c, c, ((0,), (0,)))


def first_inverse_kernel(x_ref, y_ref, gc_ref, gb_out, inv_out, inv_ref):
    gram_b = x_ref[:, :64] + y_ref[:, :64]
    gb_out[...] = gram_b
    invert_into(inv_ref, gram_b * gc_ref[...])
    inv_out[...] = block_diagonal(inv_ref[...])


def inverse_kernel(x_ref, y_ref, out_ref, inv_ref):
    invert_into(inv_ref, x_ref[...] * y_ref[...])
    out_ref[...] = block_diagonal(inv_ref[...])


def third_factor(depth, x_ref, y_ref, ga_ref, na_ref, inv_ref):
    total = x_ref[...] + y_ref[...]
    raw = total[depth:, :64]
    row, col = column_norms(raw)
    gram_b = raw / (row * col)
    invert_into(inv_ref, gram_b * ga_ref[...])
    three = (total[:depth, :64] + total[:depth, 64:]) / (na_ref[...] * row)
    return dot(three, inv_ref[...]), gram_b, row, col


def last_kernel(x_ref, y_ref, ga_ref, na_ref, bt_ref, a_ref, c_out, b_out, a_out, inv_ref):
    c, _, _, col = third_factor(c_out.shape[0], x_ref, y_ref, ga_ref, na_ref, inv_ref)
    c_out[...] = c
    b_out[...] = bt_ref[...] / col
    a_out[...] = a_ref[...] / wide(na_ref[...])


def place():
    ja = lax.axis_index("ja")
    return lax.rem(ja, 2), lax.div(ja, 2)


def add_kernel(*refs):
    parts = [r[...] for r in refs[:-1]]
    while len(parts) > 1:
        parts = [parts[i] + parts[i + 1] for i in range(0, len(parts), 2)]
    refs[-1][...] = parts[0]


def contract(stored_ref, scaled, keep_ref, send_ref):
    depth, rows, _ = stored_ref.shape
    part = rows // 2
    chunk = min(64, part)
    core, _ = place()
    for out, which in ((keep_ref, core), (send_ref, 1 - core)):

        @pl.loop(0, part // chunk)
        def _(i):
            at = pl.multiple_of(which * part + i * chunk, chunk)
            total = stored_ref[0, pl.ds(at, chunk), :] * scaled[0:1, :]
            for k in range(1, depth):
                total = total + stored_ref[k, pl.ds(at, chunk), :] * scaled[k : k + 1, :]
            out[pl.ds(pl.multiple_of(i * chunk, chunk), chunk), :] = total


def contract_start_kernel(stored_ref, c_ref, keep_ref, send_ref):
    contract(stored_ref, c_ref[...], keep_ref, send_ref)


def contract_kernel(stored_ref, x_ref, y_ref, ga_ref, na_ref,
                    c_out, gb_out, gc_out, keep_ref, send_ref, inv_ref):
    c, gram_b, norm, _ = third_factor(c_out.shape[0], x_ref, y_ref, ga_ref, na_ref, inv_ref)
    c_out[...] = wide(c)
    gb_out[...] = gram_b
    gc_out[...] = dot(c, c, ((0,), (0,)))
    contract(stored_ref, wide(c / norm), keep_ref, send_ref)


def spread_kernel(keep_ref, recv_ref, own_ref, *send_refs):
    rows = own_ref.shape[0]
    _, z = place()
    for d, out in enumerate((own_ref,) + send_refs):
        at = pl.multiple_of((z ^ d) * rows, rows)
        out[...] = keep_ref[pl.ds(at, rows), :] + recv_ref[pl.ds(at, rows), :]


def gather_kernel(*refs):
    parts, out = refs[:-1], refs[-1]
    rows = parts[0].shape[0]
    _, z = place()
    for d, part in enumerate(parts):
        at = pl.multiple_of((z ^ d) * rows, rows)
        out[pl.ds(at, rows), :] = part[...]


def second_weights(bt_ref, w_ref, w8_ref):
    unit = jnp.maximum(jnp.max(jnp.abs(bt_ref[...]), axis=1, keepdims=True), TINY) / TOP
    columns = bt_ref.shape[1]
    chunk = min(128, columns)

    @pl.loop(0, columns // chunk)
    def _(i):
        here = pl.ds(pl.multiple_of(i * chunk, chunk), chunk)
        part = bt_ref[:, here]
        hi = part.astype(BF16).astype(F32)
        for out, parts in ((w_ref, (hi, part - hi)), (w8_ref, split8(part, unit))):
            b = jnp.concatenate(parts, axis=0).T
            turned = pltpu.roll(b, 64, 1)
            out[0, here, :] = b.astype(out.dtype)
            out[1, here, :] = turned.astype(out.dtype)

    return wide(row_of(unit))


def times_b(high0, high1, low0, low1, w_ref, w8_ref):
    results = []
    for first, second, weights in ((high0, high1, w_ref), (low0, low1, w8_ref)):
        x, y = dot16(first, weights[0]), dot16(second, weights[1])
        left = iota(*x.shape, 1) < 64
        results.append((jnp.where(left, x, y), pltpu.roll(jnp.where(left, y, x), 64, 1)))
    (high, high_rest), (low, low_rest) = results
    return high + high_rest, low + low_rest * 0.0625


def load_kernel(t_ref, bt_ref, high_ref, low_ref, unit_ref, stored_ref, ring, sems, w_ref, w8_ref):
    depth, _, half, columns = t_ref.shape
    slots, _, block, _ = ring.shape
    count = half // block
    steps = depth * count

    def copy(step):
        at = pl.multiple_of((step % count) * block, block)
        return pltpu.make_async_copy(
            t_ref.at[step // count, :, pl.ds(at, block), :], ring.at[step % slots], sems.at[step % slots]
        )

    for step in range(slots):
        copy(step).start()
    scale = second_weights(bt_ref, w_ref, w8_ref)

    @pl.loop(0, steps)
    def _(step):
        copy(step).wait()
        k, at = step // count, pl.multiple_of((step % count) * block, block)
        slot = step % slots
        piece = min(32, block)

        def largest(i, top):
            here = pl.ds(pl.multiple_of(i * piece, piece), piece)
            both = jnp.maximum(jnp.abs(ring[slot, 0, here, :]), jnp.abs(ring[slot, 1, here, :]))
            return jnp.maximum(top, jnp.max(both, axis=0, keepdims=True))

        top = lax.fori_loop(0, block // piece, largest, jnp.full((1, columns), TINY, F32))
        unit = jnp.full((1, 128), jnp.max(top)) / (TOP * 256.0)
        inverse = (1.0 / unit)[:, :1]
        rows = pl.ds(at, block)

        @pl.loop(0, block // piece)
        def _(i):
            here = pl.ds(pl.multiple_of(i * piece, piece), piece)
            rows = pl.ds(pl.multiple_of(at + i * piece, piece), piece)
            for h in range(2):
                t = ring[slot, h, here, :]
                hi = t.astype(BF16)
                high_ref[k, h, rows, :] = hi
                low_ref[k, h, rows, :] = ((t - hi.astype(F32)) * inverse).astype(F8)

        unit_ref[step] = unit

        @pl.when(step + slots < steps)
        def _():
            copy(step + slots).start()

        high, low = times_b(
            high_ref[k, 0, rows, :], high_ref[k, 1, rows, :],
            low_ref[k, 0, rows, :], low_ref[k, 1, rows, :], w_ref, w8_ref,
        )
        stored_ref[k, rows, :] = high + low * (scale * unit)


def pass_b_kernel(with_stored, high_ref, low_ref, unit_ref, bt_ref, gram_ref, a_ref, *refs):
    if with_stored:
        _, sums_ref, stored_ref, w_ref, w8_ref = refs
    else:
        sums_ref, w_ref, w8_ref = refs
    depth, _, half, _ = high_ref.shape
    count = unit_ref.shape[0] // depth
    block = half // count
    chunk = min(512, half)
    scale = second_weights(bt_ref, w_ref, w8_ref)
    sums_ref[:depth, :] = jnp.zeros((depth, 128), F32)
    sums_ref[depth:, :] = gram_ref[...]

    @pl.loop(0, depth)
    def _(k):
        sums = jnp.zeros((1, 128), F32)
        for q in range(0, half, chunk):
            rows = slice(q, q + chunk)
            high, low = times_b(
                high_ref[k, 0, rows, :], high_ref[k, 1, rows, :],
                low_ref[k, 0, rows, :], low_ref[k, 1, rows, :], w_ref, w8_ref,
            )
            for at in range(0, chunk, block):
                here = slice(at, at + block)
                unit = unit_ref[k * count + (q + at) // block]
                total = high[here] + low[here] * (scale * unit)
                if with_stored:
                    stored_ref[k, q + at : q + at + block, :] = total
                sums += jnp.sum(total * a_ref[q + at : q + at + block, :], axis=0, keepdims=True)
        sums_ref[:depth, :] += jnp.where(iota(depth, 128, 0) == k, sums, 0.0)


def pass_a_kernel(high_ref, low_ref, unit_ref, half_ref, other_ref, inv_ref, c_ref,
                  a_out, first_out, second_out, w_ref, w8_ref, acc_ref):
    depth, _, half, columns = high_ref.shape
    count = unit_ref.shape[0] // depth
    block = half // count
    part = half // 2
    core, _ = place()
    inv = inv_ref[...]
    a_out[pl.ds(pl.multiple_of(core * part, part), part), :] = dot(half_ref[...], inv)
    a_out[pl.ds(pl.multiple_of((1 - core) * part, part), part), :] = dot(other_ref[...], inv)
    at = a_out[...].T
    gram = dot(at, at, ((1,), (1,)))
    gram = wide(gram[:64, :64] + gram[64:, 64:])
    top = jnp.max(jnp.abs(at), axis=1, keepdims=True)
    unit = jnp.maximum(jnp.maximum(top[:64], top[64:]), TINY) / TOP
    for h in range(2):
        rows = at[64 * h : 64 * h + 64]
        hi, lo = split(rows)
        w_ref[h, :64, :] = hi
        w_ref[h, 64:, :] = lo
        hi8, lo8 = split8(rows, unit)
        w8_ref[h, :64, :] = hi8.astype(F8)
        w8_ref[h, 64:, :] = lo8.astype(F8)
    units = jnp.concatenate([unit, unit * 0.0625], axis=0)
    acc_ref[...] = jnp.zeros_like(acc_ref)

    @pl.loop(0, depth)
    def _(k):
        row = jnp.sum(jnp.where(iota(depth, 128, 0) == k, c_ref[...], 0.0), axis=0, keepdims=True)
        col = col_of(row[:, :64])
        col = jnp.concatenate([col, col], axis=0)
        acc_ref[...] += col * (dot16(w_ref[0], high_ref[k, 0]) + dot16(w_ref[1], high_ref[k, 1]))
        for b in range(count):
            rows = slice(b * block, b * block + block)
            low = dot16(w8_ref[0, :, rows], low_ref[k, 0, rows, :])
            low += dot16(w8_ref[1, :, rows], low_ref[k, 1, rows, :])
            acc_ref[...] += (col * units * unit_ref[k * count + b][:, :1]) * low

    total = acc_ref[:64, :] + acc_ref[64:, :]
    first_out[:, :columns] = total[:32]
    second_out[:, :columns] = total[32:]
    first_out[:, columns:] = gram[:32]
    second_out[:, columns:] = gram[32:]


def solve_b_kernel(share, a0_ref, a1_ref, b0_ref, b1_ref, gc_ref, bt_out, gb_out, ga_out, na_out, inv_ref):
    total = jnp.concatenate([a0_ref[...] + a1_ref[...], b0_ref[...] + b1_ref[...]], axis=0)
    columns = bt_out.shape[1]
    raw = total[:, columns : columns + 64]
    row, col = column_norms(raw)
    gram_a = raw / (row * col)
    invert_into(inv_ref, gram_a * gc_ref[...])
    bt = dot(inv_ref[...], total[:, :columns] / col)
    bt_out[...] = bt
    gb_out[...] = wide(dot(bt, bt, ((1,), (1,)))) * share
    ga_out[...] = gram_a
    na_out[...] = row


def call(kernel, outs, *operands, scratch=(), mib=2, name=None, flops=200000, nbytes=200000, first=VMEM, keep=(), written=()):
    going = [operands[i] for i in keep + written]
    results, held = len(outs), len(keep)

    def run(*refs):
        rest = refs[len(operands) :]
        kernel(*refs[: len(operands)], *rest[:results], *rest[results + held :])

    return pl.pallas_call(
        run,
        in_specs=[first] + [VMEM] * (len(operands) - 1),
        out_specs=[VMEM] * (results + len(going)),
        out_shape=outs + [pltpu.VMEM(x.shape, x.dtype) for x in going],
        scratch_shapes=scratch,
        input_output_aliases={i: results + n for n, i in enumerate(keep + written)},
        compiler_params=params(mib),
        cost_estimate=cost(flops, nbytes),
        name=name,
    )(*operands)


def resident(x):
    return pltpu.with_memory_space_constraint(x, pltpu.VMEM)


def add(*parts):
    return call(add_kernel, [shape(*parts[0].shape)], *parts, name="add")[0]


def inverse_space():
    return [pltpu.VMEM((64, 64), F32)]


def weights_space(columns):
    return [pltpu.VMEM((2, columns, 128), BF16), pltpu.VMEM((2, columns, 128), F8)]


def load(tensor, bt):
    depth, rows, columns = tensor.shape
    half = rows // 2
    block = min(256, half)
    return call(
        load_kernel,
        [
            pltpu.VMEM((depth, 2, half, columns), BF16),
            pltpu.VMEM((depth, 2, half, columns), F8),
            shape(depth * (half // block), 1, 128),
            pltpu.VMEM((depth, half, 128), F32),
        ],
        tensor.reshape(depth, 2, half, columns), bt,
        first=pl.BlockSpec(memory_space=pl.ANY),
        scratch=[
            pltpu.VMEM((2, 2, block, columns), F32), pltpu.SemaphoreType.DMA((2,)),
        ] + weights_space(columns),
        mib=8, name="load", flops=6 * tensor.size * 64, nbytes=4 * tensor.size,
    )


def pass_a(kept, half, other, inv, c):
    depth, _, rows, columns = kept[0].shape
    *outs, high, low = call(
        pass_a_kernel,
        [shape(rows, 128), shape(32, columns + 128), shape(32, columns + 128)],
        resident(kept[0]), resident(kept[1]), kept[2], half, other, inv, c,
        scratch=[
            pltpu.VMEM((2, 128, rows), BF16), pltpu.VMEM((2, 128, rows), F8),
            pltpu.VMEM((128, columns), F32),
        ],
        mib=8, name="pass_a", flops=6 * kept[0].size * 64, nbytes=3 * kept[0].size, keep=(0, 1),
    )
    return outs, [high, low, kept[2]]


def pass_b(kept, stored, bt, gram, a, last):
    depth, _, rows, columns = kept[0].shape
    sums, *rest = call(
        functools.partial(pass_b_kernel, not last), [shape(depth + 64, 128)],
        resident(kept[0]), resident(kept[1]), kept[2], bt, gram, a, *([] if last else [resident(stored)]),
        scratch=weights_space(columns),
        mib=8, name="pass_b", flops=6 * kept[0].size * 64, nbytes=3 * kept[0].size,
        keep=() if last else (0, 1), written=() if last else (6,),
    )
    if last:
        return sums, kept, stored
    return sums, [rest[0], rest[1], kept[2]], rest[2]


def across(x, axis, mask):
    n = lax.axis_size(axis)
    return lax.ppermute(x, axis, [(i, i ^ mask) for i in range(n)])


def masks(axis):
    return [(axis, 1 << b) for b in range(lax.axis_size(axis).bit_length() - 1)]


def butterfly(x, steps):
    for axis, mask in steps[:-1]:
        x = add(x, across(x, axis, mask))
    axis, mask = steps[-1]
    return x, across(x, axis, mask)


def body(tensor, b_init, c_init):
    depth, rows, columns = tensor.shape
    half = rows // 2
    n_ia, n_ja = lax.axis_size("ia"), lax.axis_size("ja")
    n_z = n_ja // 2
    ja = lax.axis_index("ja")
    piece = half // 2 // n_z

    everyone = masks("ja") + masks("ia")
    bt, gram, c, gram_c = call(
        functools.partial(start_kernel, 1.0),
        [shape(64, columns), shape(64, 128), shape(depth, 128), shape(64, 64)],
        b_init, c_init, name="start",
    )
    *kept, stored = load(tensor, bt)
    def sum_over_ja(keep, send, grams):
        recv = across(send, "ja", 1)
        if len(grams) == 2:
            (inv,) = call(inverse_kernel, [shape(128, 128)], *grams, scratch=inverse_space(), name="inverse")
            keep, inv = lax.optimization_barrier((keep, inv))
        own, *sends = call(
            spread_kernel, [shape(piece, 128)] * n_z, keep, recv, mib=2, name="spread"
        )
        own = add(own, *[across(s, "ja", 2 * d) for d, s in enumerate(sends, 1)])
        parts = [own] + [across(own, "ja", 2 * d) for d in range(1, n_z)]
        (mine,) = call(gather_kernel, [shape(half // 2, 128)], *parts, mib=2, name="gather")
        gram_b = None
        if len(grams) == 3:
            gram_b, inv = call(
                first_inverse_kernel, [shape(64, 64), shape(128, 128)], *grams,
                scratch=inverse_space(), name="inverse",
            )
        return mine, across(mine, "ja", 1), inv

    def sum_over_ia(first, second):
        order = masks("ia")
        return butterfly(first, order) + butterfly(second, order[1:] + order[:1])

    keep, send = call(
        contract_start_kernel, [shape(half // 2, 128)] * 2, resident(stored), c,
        name="contract", flops=stored.size * 2, nbytes=stored.size * 4,
    )
    grams = butterfly(gram, masks("ja")) + (gram_c,)
    for sweep in range(SWEEPS):
        last = sweep == SWEEPS - 1
        mine, other, inv = sum_over_ja(keep, send, grams)
        (a, first, second), kept = pass_a(kept, mine, other, inv, c)
        bt, gram, gram_a, norm_a = call(
            functools.partial(solve_b_kernel, 1.0 / n_ia),
            [shape(64, columns), shape(64, 128), shape(64, 64), shape(1, 64)],
            *sum_over_ia(first, second), gram_c, scratch=inverse_space(), name="solve_b",
        )
        sums, kept, stored = pass_b(kept, stored, bt, gram, a, last)
        sums = butterfly(sums, everyone)
        if last:
            break
        c, gram_b, gram_c, keep, send = call(
            contract_kernel,
            [shape(depth, 128), shape(64, 64), shape(64, 64)] + [shape(half // 2, 128)] * 2,
            resident(stored), *sums, gram_a, norm_a, scratch=inverse_space(),
            name="contract", flops=stored.size * 2, nbytes=stored.size * 4,
        )
        grams = (gram_b, gram_c)
    factor_c, bt, a = call(
        last_kernel, [shape(depth, 64), shape(64, columns), shape(half, 128)],
        *sums, gram_a, norm_a, bt, a, scratch=inverse_space(), name="last",
    )
    share = rows // n_ja
    at = ja * share
    mine = lax.dynamic_slice_in_dim(a, at % half, share, 0)
    factor_a = jnp.where(at < half, mine[:, :64], mine[:, 64:])
    return factor_a, bt.T, factor_c


def solution(mesh):
    in_specs = (P(None, "ia", "ja"), P("ja", None), P())
    out_specs = (P(("ia", "ja"), None), P("ja", None), P())
    return jax.shard_map(body, mesh=mesh, in_specs=in_specs, out_specs=out_specs, check_vma=False)
```

```python
import functools

import jax
import jax.numpy as jnp
from jax import lax
from jax.experimental import pallas as pl
from jax.experimental.pallas import tpu as pltpu
from jax.sharding import PartitionSpec as P

SWEEPS = 4
EPS = 1e-6
HIGH = lax.Precision.HIGHEST
F32 = jnp.float32
BF16 = jnp.bfloat16
F8 = jnp.float8_e4m3fn
TOP = 224.0
TINY = 1e-30
GROUPS = 4
VMEM = pl.BlockSpec(memory_space=pltpu.VMEM)
MIB = 1 << 20


def params(mib):
    return pltpu.CompilerParams(vmem_limit_bytes=mib * MIB)


def cost(flops, nbytes):
    return pl.CostEstimate(flops=int(flops), bytes_accessed=int(nbytes), transcendentals=0)


def shape(*dims, dtype=F32):
    return jax.ShapeDtypeStruct(dims, dtype)


def dot(a, b, dims=((1,), (0,))):
    return lax.dot_general(a, b, (dims, ((), ())), precision=HIGH, preferred_element_type=F32)


def dot16(a, b):
    return jnp.dot(a, b, preferred_element_type=F32)


def split(x):
    hi = x.astype(BF16)
    return hi, (x - hi.astype(F32)).astype(BF16)


def iota(rows, cols, dim):
    return lax.broadcasted_iota(jnp.int32, (rows, cols), dim)


def eye(n):
    return (iota(n, n, 0) == iota(n, n, 1)).astype(F32)


def column_norms(raw):
    diagonal = raw * eye(raw.shape[0])
    row = jnp.sqrt(jnp.sum(diagonal, axis=0, keepdims=True) + EPS)
    col = jnp.sqrt(jnp.sum(diagonal, axis=1, keepdims=True) + EPS)
    return row, col


def eliminate(g):
    n = g.shape[0]
    m = jnp.concatenate([g, eye(n)], axis=1)
    rows = iota(n, 2 * n, 0)
    for k in range(n):
        pivot = m[k : k + 1, :] / m[k : k + 1, k : k + 1]
        m = jnp.where(rows == k, pivot, m - m[:, k : k + 1] * pivot)
    return m[:, n:]


def invert_into(out_ref, g):
    n = g.shape[0]
    one = eye(n)
    diagonal = g * one
    row = lax.rsqrt(jnp.sum(diagonal, axis=0, keepdims=True))
    col = lax.rsqrt(jnp.sum(diagonal, axis=1, keepdims=True))
    power = one - g * (row * col)
    close = jnp.sum(power * power) <= 0.25

    @pl.when(close)
    def _():
        e = power
        total = one + e
        for _ in range(4):
            e = dot(e, e)
            total = total + dot(total, e)
        out_ref[...] = total * (row * col)

    @pl.when(jnp.logical_not(close))
    def _():
        out_ref[...] = eliminate(g)


def block_diagonal(g):
    zero = jnp.zeros_like(g)
    return jnp.concatenate(
        [jnp.concatenate([g, zero], axis=1), jnp.concatenate([zero, g], axis=1)], axis=0
    )


def wide(x):
    return jnp.concatenate([x, x], axis=1)


def row_of(col):
    return jnp.sum(eye(col.shape[0]) * col, axis=0, keepdims=True)


def col_of(row):
    return jnp.sum(eye(row.shape[1]) * row, axis=1, keepdims=True)


def split8(x, unit):
    x = x / unit
    hi = x.astype(F8).astype(F32)
    return hi, ((x - hi) * 16.0).astype(F8).astype(F32)


def start_kernel(share, b_ref, c_ref, bt_ref, gb_ref, c_out, gc_ref):
    b = b_ref[...]
    bt_ref[...] = b.T
    gb_ref[...] = wide(dot(b, b, ((0,), (0,))))
    c = c_ref[...]
    c_out[...] = wide(c)
    gc_ref[...] = dot(c, c, ((0,), (0,)))


def first_inverse_kernel(x_ref, y_ref, gc_ref, gb_out, inv_out, inv_ref):
    gram_b = x_ref[:, :64] + y_ref[:, :64]
    gb_out[...] = gram_b
    invert_into(inv_ref, gram_b * gc_ref[...])
    inv_out[...] = block_diagonal(inv_ref[...])


def inverse_kernel(x_ref, y_ref, out_ref, inv_ref):
    invert_into(inv_ref, x_ref[...] * y_ref[...])
    out_ref[...] = block_diagonal(inv_ref[...])


def third_factor(depth, x_ref, y_ref, ga_ref, na_ref, inv_ref):
    total = x_ref[...] + y_ref[...]
    raw = total[:, :64]
    row, col = column_norms(raw)
    gram_b = raw / (row * col)
    invert_into(inv_ref, gram_b * ga_ref[...])
    three = total.T[64 : 64 + depth, :] / (na_ref[...] * row)
    return dot(three, inv_ref[...]), gram_b, row, col


def last_kernel(x_ref, y_ref, ga_ref, na_ref, bt_ref, a_ref, c_out, b_out, a_out, inv_ref):
    c, _, _, col = third_factor(c_out.shape[0], x_ref, y_ref, ga_ref, na_ref, inv_ref)
    c_out[...] = c
    b_out[...] = bt_ref[...] / col
    a_out[...] = a_ref[...] / wide(na_ref[...])


def place():
    ja = lax.axis_index("ja")
    return lax.rem(ja, 2), lax.div(ja, 2)


def add_kernel(*refs):
    parts = [r[...] for r in refs[:-1]]
    while len(parts) > 1:
        parts = [parts[i] + parts[i + 1] for i in range(0, len(parts), 2)]
    refs[-1][...] = parts[0]


def contract(stored_refs, scaled, keep_ref, send_ref):
    depth = scaled.shape[0]
    group = depth // len(stored_refs)
    part = stored_refs[0].shape[1] // 2
    chunk = min(64, part)
    core, _ = place()
    for out, which in ((keep_ref, core), (send_ref, 1 - core)):

        @pl.loop(0, part // chunk)
        def _(i):
            at = pl.multiple_of(which * part + i * chunk, chunk)
            total = None
            for k in range(depth):
                term = stored_refs[k // group][k % group, pl.ds(at, chunk), :] * scaled[k : k + 1, :]
                total = term if total is None else total + term
            out[pl.ds(pl.multiple_of(i * chunk, chunk), chunk), :] = total


def contract_start_kernel(c_ref, *refs):
    contract(refs[:GROUPS], c_ref[...], *refs[GROUPS:])


def contract_kernel(x_ref, y_ref, ga_ref, na_ref, *refs):
    c_out, gb_out, gc_out, keep_ref, send_ref, inv_ref = refs[GROUPS:]
    c, gram_b, norm, _ = third_factor(c_out.shape[0], x_ref, y_ref, ga_ref, na_ref, inv_ref)
    c_out[...] = wide(c)
    gb_out[...] = gram_b
    gc_out[...] = dot(c, c, ((0,), (0,)))
    contract(refs[:GROUPS], wide(c / norm), keep_ref, send_ref)


def spread_kernel(keep_ref, recv_ref, own_ref, *send_refs):
    rows = own_ref.shape[0]
    _, z = place()
    for d, out in enumerate((own_ref,) + send_refs):
        at = pl.multiple_of((z ^ d) * rows, rows)
        out[...] = keep_ref[pl.ds(at, rows), :] + recv_ref[pl.ds(at, rows), :]


def gather_kernel(*refs):
    parts, out = refs[:-1], refs[-1]
    rows = parts[0].shape[0]
    _, z = place()
    for d, part in enumerate(parts):
        at = pl.multiple_of((z ^ d) * rows, rows)
        out[pl.ds(at, rows), :] = part[...]


def second_weights(bt_ref, w_ref, w8_ref):
    unit = jnp.maximum(jnp.max(jnp.abs(bt_ref[...]), axis=1, keepdims=True), TINY) / TOP
    columns = bt_ref.shape[1]
    chunk = min(128, columns)

    @pl.loop(0, columns // chunk)
    def _(i):
        here = pl.ds(pl.multiple_of(i * chunk, chunk), chunk)
        part = bt_ref[:, here]
        hi = part.astype(BF16).astype(F32)
        for out, parts in ((w_ref, (hi, part - hi)), (w8_ref, split8(part, unit))):
            b = jnp.concatenate(parts, axis=0).T
            turned = pltpu.roll(b, 64, 1)
            out[0, here, :] = b.astype(out.dtype)
            out[1, here, :] = turned.astype(out.dtype)

    return wide(row_of(unit))


def times_b(first, second, weights):
    x, y = dot16(first, weights[0]), dot16(second, weights[1])
    left = iota(*x.shape, 1) < 64
    return jnp.where(left, x, y), pltpu.roll(jnp.where(left, y, x), 64, 1)


def times_both(high0, high1, low0, low1, w_ref, w8_ref):
    high, high_rest = times_b(high0, high1, w_ref)
    low, low_rest = times_b(low0, low1, w8_ref)
    return high + high_rest, low + low_rest * 0.0625


def load_kernel(t_ref, bt_ref, high_ref, low_ref, unit_ref, *refs):
    stored_refs, (ring, sems, w_ref, w8_ref) = refs[:GROUPS], refs[GROUPS:]
    depth, _, half, columns = t_ref.shape
    slots, _, block, _ = ring.shape
    count = half // block
    steps = depth * count

    def copy(step):
        at = pl.multiple_of((step % count) * block, block)
        return pltpu.make_async_copy(
            t_ref.at[step // count, :, pl.ds(at, block), :], ring.at[step % slots], sems.at[step % slots]
        )

    for step in range(slots):
        copy(step).start()
    scale = second_weights(bt_ref, w_ref, w8_ref)

    @pl.loop(0, steps)
    def _(step):
        copy(step).wait()
        k, at = step // count, pl.multiple_of((step % count) * block, block)
        slot = step % slots
        piece = min(64, block)
        rows = pl.ds(at, block)

        def convert(i, top):
            here = pl.ds(pl.multiple_of(i * piece, piece), piece)
            there = pl.ds(pl.multiple_of(at + i * piece, piece), piece)
            for h in range(2):
                t = ring[slot, h, here, :]
                high_ref[k, h, there, :] = t.astype(BF16)
                top = jnp.maximum(top, jnp.max(jnp.abs(t).reshape(piece // 8, 8, columns), axis=0))
            return top

        top = lax.fori_loop(0, block // piece, convert, jnp.full((8, columns), TINY, F32))
        unit = jnp.full((1, 128), jnp.max(top)) / (TOP * 256.0)
        inverse = (1.0 / unit)[:, :1]
        unit_ref[step] = unit
        high, rest = times_b(high_ref[k, 0, rows, :], high_ref[k, 1, rows, :], w_ref)
        high = high + rest

        @pl.loop(0, block // piece)
        def _(i):
            here = pl.ds(pl.multiple_of(i * piece, piece), piece)
            there = pl.ds(pl.multiple_of(at + i * piece, piece), piece)
            for h in range(2):
                t = ring[slot, h, here, :]
                low_ref[k, h, there, :] = ((t - t.astype(BF16).astype(F32)) * inverse).astype(F8)

        @pl.when(step + slots < steps)
        def _():
            copy(step + slots).start()

        low, rest = times_b(low_ref[k, 0, rows, :], low_ref[k, 1, rows, :], w8_ref)
        total = high + (low + rest * 0.0625) * (scale * unit)
        group = depth // GROUPS
        for g, stored_ref in enumerate(stored_refs):

            @pl.when(k // group == g)
            def _(stored_ref=stored_ref):
                stored_ref[k % group, rows, :] = total


def weights_kernel(bt_ref, w_ref, w8_ref, scale_ref):
    scale_ref[...] = second_weights(bt_ref, w_ref, w8_ref)


def pass_b_kernel(first, depth, high_ref, low_ref, unit_ref, w_ref, w8_ref, scale_ref, _, stored_ref):
    half = high_ref.shape[2]
    count = unit_ref.shape[0] // depth
    block = half // count
    chunk = min(512, half)

    @pl.loop(0, stored_ref.shape[0])
    def _(i):
        k = first + i
        for q in range(0, half, chunk):
            rows = slice(q, q + chunk)
            high, low = times_both(
                high_ref[k, 0, rows, :], high_ref[k, 1, rows, :],
                low_ref[k, 0, rows, :], low_ref[k, 1, rows, :], w_ref, w8_ref,
            )
            for at in range(0, chunk, block):
                here = slice(at, at + block)
                unit = unit_ref[k * count + (q + at) // block]
                stored_ref[i, q + at : q + at + block, :] = high[here] + low[here] * (scale_ref[...] * unit)


def pass_a_kernel(high_ref, low_ref, unit_ref, half_ref, other_ref, inv_ref, c_ref,
                  a_out, p_out, first_out, second_out, w_ref, w8_ref, acc_ref):
    depth, _, half, columns = high_ref.shape
    count = unit_ref.shape[0] // depth
    block = half // count
    part = half // 2
    core, _ = place()
    inv = inv_ref[...]
    a_out[pl.ds(pl.multiple_of(core * part, part), part), :] = dot(half_ref[...], inv)
    a_out[pl.ds(pl.multiple_of((1 - core) * part, part), part), :] = dot(other_ref[...], inv)
    at = a_out[...].T
    gram = dot(at, at, ((1,), (1,)))
    gram = wide(gram[:64, :64] + gram[64:, 64:])
    top = jnp.max(jnp.abs(at), axis=1, keepdims=True)
    unit = jnp.maximum(jnp.maximum(top[:64], top[64:]), TINY) / TOP
    for h in range(2):
        rows = at[64 * h : 64 * h + 64]
        hi, lo = split(rows)
        w_ref[h, :64, :] = hi
        w_ref[h, 64:, :] = lo
        hi8, lo8 = split8(rows, unit)
        w8_ref[h, :64, :] = hi8.astype(F8)
        w8_ref[h, 64:, :] = lo8.astype(F8)
    units = jnp.concatenate([unit, unit * 0.0625], axis=0)
    acc_ref[...] = jnp.zeros_like(acc_ref)

    @pl.loop(0, depth)
    def _(k):
        row = jnp.sum(jnp.where(iota(depth, 128, 0) == k, c_ref[...], 0.0), axis=0, keepdims=True)
        col = col_of(row[:, :64])
        both = dot16(w_ref[0], high_ref[k, 0]) + dot16(w_ref[1], high_ref[k, 1])
        for b in range(count):
            rows = slice(b * block, b * block + block)
            low = dot16(w8_ref[0, :, rows], low_ref[k, 0, rows, :])
            low += dot16(w8_ref[1, :, rows], low_ref[k, 1, rows, :])
            both += (units * unit_ref[k * count + b][:, :1]) * low
        product = both[:64] + both[64:]
        p_out[k] = product
        acc_ref[...] += col * product

    total = acc_ref[...]
    first_out[:, :columns] = total[:32]
    second_out[:, :columns] = total[32:]
    first_out[:, columns:] = gram[:32]
    second_out[:, columns:] = gram[32:]


def solve_b_kernel(share, a0_ref, a1_ref, b0_ref, b1_ref, gc_ref, p_ref, bt_out, sums_out, ga_out, na_out, inv_ref):
    total = jnp.concatenate([a0_ref[...] + a1_ref[...], b0_ref[...] + b1_ref[...]], axis=0)
    columns = bt_out.shape[1]
    raw = total[:, columns : columns + 64]
    row, col = column_norms(raw)
    gram_a = raw / (row * col)
    invert_into(inv_ref, gram_a * gc_ref[...])
    bt = dot(inv_ref[...], total[:, :columns] / col)
    bt_out[...] = bt
    sums = wide(dot(bt, bt, ((1,), (1,)))) * share
    lane = iota(64, 128, 1)
    for k in range(p_ref.shape[0]):
        sums = jnp.where(lane == 64 + k, jnp.sum(bt * p_ref[k], axis=1, keepdims=True), sums)
    sums_out[...] = sums
    ga_out[...] = gram_a
    na_out[...] = row


def call(kernel, outs, *operands, scratch=(), mib=2, name=None, flops=200000, nbytes=200000, first=VMEM, keep=(), written=()):
    going = [operands[i] for i in keep + written]
    results, held = len(outs), len(keep)

    def run(*refs):
        rest = refs[len(operands) :]
        kernel(*refs[: len(operands)], *rest[:results], *rest[results + held :])

    return pl.pallas_call(
        run,
        in_specs=[first] + [VMEM] * (len(operands) - 1),
        out_specs=[VMEM] * (results + len(going)),
        out_shape=outs + [pltpu.VMEM(x.shape, x.dtype) for x in going],
        scratch_shapes=scratch,
        input_output_aliases={i: results + n for n, i in enumerate(keep + written)},
        compiler_params=params(mib),
        cost_estimate=cost(flops, nbytes),
        name=name,
    )(*operands)


def resident(x):
    return pltpu.with_memory_space_constraint(x, pltpu.VMEM)


def add(*parts):
    return call(add_kernel, [shape(*parts[0].shape)], *parts, name="add")[0]


def inverse_space():
    return [pltpu.VMEM((64, 64), F32)]


def weights_space(columns):
    return [pltpu.VMEM((2, columns, 128), BF16), pltpu.VMEM((2, columns, 128), F8)]


def load(tensor, bt):
    depth, rows, columns = tensor.shape
    half = rows // 2
    block = min(256, half)
    return call(
        load_kernel,
        [
            pltpu.VMEM((depth, 2, half, columns), BF16),
            pltpu.VMEM((depth, 2, half, columns), F8),
            shape(depth * (half // block), 1, 128),
        ] + [pltpu.VMEM((depth // GROUPS, half, 128), F32)] * GROUPS,
        tensor.reshape(depth, 2, half, columns), bt,
        first=pl.BlockSpec(memory_space=pl.ANY),
        scratch=[
            pltpu.VMEM((2, 2, block, columns), F32), pltpu.SemaphoreType.DMA((2,)),
        ] + weights_space(columns),
        mib=7, name="load", flops=6 * tensor.size * 64, nbytes=4 * tensor.size,
    )


def pass_a(kept, half, other, inv, c):
    depth, _, rows, columns = kept[0].shape
    *outs, high, low = call(
        pass_a_kernel,
        [shape(rows, 128), shape(depth, 64, columns)] + [shape(32, columns + 128)] * 2,
        resident(kept[0]), resident(kept[1]), kept[2], half, other, inv, c,
        scratch=[
            pltpu.VMEM((2, 128, rows), BF16), pltpu.VMEM((2, 128, rows), F8),
            pltpu.VMEM((64, columns), F32),
        ],
        mib=7, name="pass_a", flops=6 * kept[0].size * 64, nbytes=3 * kept[0].size, keep=(0, 1),
    )
    return outs, [high, low, kept[2]]


def pass_b(kept, stored, bt):
    depth, _, rows, columns = kept[0].shape
    weights = call(
        weights_kernel,
        [shape(2, columns, 128, dtype=BF16), shape(2, columns, 128, dtype=F8), shape(1, 128)],
        bt, name="weights",
    )
    results = []
    for g, old in enumerate(stored):
        size = kept[0].size // GROUPS
        high, low, new = call(
            functools.partial(pass_b_kernel, g * old.shape[0], depth), [],
            resident(kept[0]), resident(kept[1]), kept[2], *weights, resident(old),
            mib=7, name="pass_b", flops=6 * size * 64, nbytes=3 * size, keep=(0, 1), written=(6,),
        )
        kept = [high, low, kept[2]]
        results.append(new)
    return kept, results


def across(x, axis, mask):
    n = lax.axis_size(axis)
    return lax.ppermute(x, axis, [(i, i ^ mask) for i in range(n)])


def masks(axis):
    return [(axis, 1 << b) for b in range(lax.axis_size(axis).bit_length() - 1)]


def butterfly(x, steps):
    for axis, mask in steps[:-1]:
        x = add(x, across(x, axis, mask))
    axis, mask = steps[-1]
    return x, across(x, axis, mask)


def body(tensor, b_init, c_init):
    depth, rows, columns = tensor.shape
    half = rows // 2
    n_ia, n_ja = lax.axis_size("ia"), lax.axis_size("ja")
    n_z = n_ja // 2
    ja = lax.axis_index("ja")
    piece = half // 2 // n_z

    everyone = masks("ja") + masks("ia")
    bt, gram, c, gram_c = call(
        functools.partial(start_kernel, 1.0),
        [shape(64, columns), shape(64, 128), shape(depth, 128), shape(64, 64)],
        b_init, c_init, name="start",
    )
    *kept, = load(tensor, bt)
    kept, stored = kept[:3], kept[3:]
    def sum_over_ja(keep, send, grams):
        recv = across(send, "ja", 1)
        if len(grams) == 2:
            (inv,) = call(inverse_kernel, [shape(128, 128)], *grams, scratch=inverse_space(), name="inverse")
            keep, inv = lax.optimization_barrier((keep, inv))
        own, *sends = call(
            spread_kernel, [shape(piece, 128)] * n_z, keep, recv, mib=2, name="spread"
        )
        own = add(own, *[across(s, "ja", 2 * d) for d, s in enumerate(sends, 1)])
        parts = [own] + [across(own, "ja", 2 * d) for d in range(1, n_z)]
        (mine,) = call(gather_kernel, [shape(half // 2, 128)], *parts, mib=2, name="gather")
        gram_b = None
        if len(grams) == 3:
            gram_b, inv = call(
                first_inverse_kernel, [shape(64, 64), shape(128, 128)], *grams,
                scratch=inverse_space(), name="inverse",
            )
        return mine, across(mine, "ja", 1), inv

    def sum_over_ia(first, second):
        order = masks("ia")
        return butterfly(first, order) + butterfly(second, order[1:] + order[:1])

    keep, send = call(
        contract_start_kernel, [shape(half // 2, 128)] * 2, c, *[resident(x) for x in stored],
        name="contract", flops=tensor.size // 8, nbytes=tensor.size // 4,
    )
    grams = butterfly(gram, masks("ja")) + (gram_c,)
    for sweep in range(SWEEPS):
        last = sweep == SWEEPS - 1
        mine, other, inv = sum_over_ja(keep, send, grams)
        (a, products, first, second), kept = pass_a(kept, mine, other, inv, c)
        bt, sums, gram_a, norm_a = call(
            functools.partial(solve_b_kernel, 1.0 / n_ia),
            [shape(64, columns), shape(64, 128), shape(64, 64), shape(1, 64)],
            *sum_over_ia(first, second), gram_c, products, scratch=inverse_space(), name="solve_b",
        )
        sums = butterfly(sums, everyone)
        if last:
            break
        kept, stored = pass_b(kept, stored, bt)
        c, gram_b, gram_c, keep, send = call(
            contract_kernel,
            [shape(depth, 128), shape(64, 64), shape(64, 64)] + [shape(half // 2, 128)] * 2,
            *sums, gram_a, norm_a, *[resident(x) for x in stored], scratch=inverse_space(),
            name="contract", flops=tensor.size // 8, nbytes=tensor.size // 4,
        )
        grams = (gram_b, gram_c)
    factor_c, bt, a = call(
        last_kernel, [shape(depth, 64), shape(64, columns), shape(half, 128)],
        *sums, gram_a, norm_a, bt, a, scratch=inverse_space(), name="last",
    )
    share = rows // n_ja
    at = ja * share
    mine = lax.dynamic_slice_in_dim(a, at % half, share, 0)
    factor_a = jnp.where(at < half, mine[:, :64], mine[:, 64:])
    return factor_a, bt.T, factor_c


def solution(mesh):
    in_specs = (P(None, "ia", "ja"), P("ja", None), P())
    out_specs = (P(("ia", "ja"), None), P("ja", None), P())
    return jax.shard_map(body, mesh=mesh, in_specs=in_specs, out_specs=out_specs, check_vma=False)
```

```python
import functools

import jax
import jax.numpy as jnp
from jax import lax
from jax.experimental import pallas as pl
from jax.experimental.pallas import tpu as pltpu
from jax.sharding import PartitionSpec as P

SWEEPS = 4
EPS = 1e-6
HIGH = lax.Precision.HIGHEST
F32 = jnp.float32
BF16 = jnp.bfloat16
F8 = jnp.float8_e4m3fn
TOP = 224.0
TINY = 1e-30
GROUPS = 4
SLOTS = 4
SPACE = 6.5
SOLVE = 3
VMEM = pl.BlockSpec(memory_space=pltpu.VMEM)
MIB = 1 << 20


def params(mib):
    return pltpu.CompilerParams(vmem_limit_bytes=int(mib * MIB))


def cost(flops, nbytes):
    return pl.CostEstimate(flops=int(flops), bytes_accessed=int(nbytes), transcendentals=0)


def shape(*dims, dtype=F32):
    return jax.ShapeDtypeStruct(dims, dtype)


def dot(a, b, dims=((1,), (0,))):
    return lax.dot_general(a, b, (dims, ((), ())), precision=HIGH, preferred_element_type=F32)


def dot16(a, b):
    return jnp.dot(a, b, preferred_element_type=F32)


def split(x):
    hi = x.astype(BF16)
    return hi, (x - hi.astype(F32)).astype(BF16)


def iota(rows, cols, dim):
    return lax.broadcasted_iota(jnp.int32, (rows, cols), dim)


def eye(n):
    return (iota(n, n, 0) == iota(n, n, 1)).astype(F32)


def column_norms(raw):
    diagonal = raw * eye(raw.shape[0])
    row = jnp.sqrt(jnp.sum(diagonal, axis=0, keepdims=True) + EPS)
    col = jnp.sqrt(jnp.sum(diagonal, axis=1, keepdims=True) + EPS)
    return row, col


def eliminate(g):
    n = g.shape[0]
    m = jnp.concatenate([g, eye(n)], axis=1)
    rows = iota(n, 2 * n, 0)
    for k in range(n):
        pivot = m[k : k + 1, :] / m[k : k + 1, k : k + 1]
        m = jnp.where(rows == k, pivot, m - m[:, k : k + 1] * pivot)
    return m[:, n:]


def invert_into(out_ref, g):
    n = g.shape[0]
    one = eye(n)
    diagonal = g * one
    row = lax.rsqrt(jnp.sum(diagonal, axis=0, keepdims=True))
    col = lax.rsqrt(jnp.sum(diagonal, axis=1, keepdims=True))
    power = one - g * (row * col)
    close = jnp.sum(power * power) <= 0.25

    @pl.when(close)
    def _():
        e = power
        total = one + e
        for _ in range(4):
            e = dot(e, e)
            total = total + dot(total, e)
        out_ref[...] = total * (row * col)

    @pl.when(jnp.logical_not(close))
    def _():
        out_ref[...] = eliminate(g)


def wide(x):
    return jnp.concatenate([x, x], axis=1)


def col_of(x, k):
    return jnp.sum(jnp.where(iota(*x.shape, 1) == k, x, 0.0), axis=1, keepdims=True)


def split8(x, unit):
    x = x / unit
    hi = x.astype(F8)
    return hi, ((x - hi.astype(F32)) * 16.0).astype(F8)


def place():
    ja = lax.axis_index("ja")
    return lax.rem(ja, 2), lax.div(ja, 2)


def factor_parts(x, w_ref, w8_ref):
    unit = jnp.maximum(jnp.max(jnp.abs(x), axis=1, keepdims=True), TINY) / TOP
    w_ref[:64, :], w_ref[64:, :] = split(x)
    w8_ref[:64, :], w8_ref[64:, :] = split8(x, unit)
    return jnp.concatenate([unit, unit * 0.0625], axis=0)


def halves(x):
    return x[:64] + x[64:]


def start_kernel(bt_ref, c_ref, sums_out, ct_out, gc_out, w_out, w8_out, scale_out):
    bt = bt_ref[...]
    depth = c_ref.shape[0]
    sums_out[...] = wide(dot(bt, bt, ((1,), (1,))))
    ct = dot(c_ref[...], (iota(depth, 128, 0) == iota(depth, 128, 1)).astype(F32), ((0,), (0,)))
    ct_out[...] = ct
    gc_out[...] = dot(ct, ct, ((1,), (1,)))
    scale_out[...] = factor_parts(bt, w_out, w8_out)


def first_inverse_kernel(x_ref, y_ref, gc_ref, gb_out, inv_out):
    gram_b = x_ref[:, :64] + y_ref[:, :64]
    gb_out[...] = gram_b
    invert_into(inv_out, gram_b * gc_ref[...])


def inverse_kernel(x_ref, y_ref, out_ref):
    invert_into(out_ref, x_ref[...] * y_ref[...])


def third_factor(depth, x_ref, y_ref, ga_ref, na_ref, inv_ref):
    total = x_ref[...] + y_ref[...]
    raw = total[:, :64]
    row, col = column_norms(raw)
    gram_b = raw / (row * col)
    invert_into(inv_ref, gram_b * ga_ref[...])
    three = jnp.where(iota(64, 128, 1) < depth, pltpu.roll(total, 64, 1), 0.0)
    return dot(inv_ref[...], three / (na_ref[...] * col)), gram_b, col


def last_kernel(x_ref, y_ref, ga_ref, na_ref, bt_ref, a_ref, ct_out, bt_out, at_out, inv_ref):
    ct, _, norm = third_factor(ct_out.shape[1], x_ref, y_ref, ga_ref, na_ref, inv_ref)
    ct_out[...] = ct[:, : ct_out.shape[1]]
    bt_out[...] = bt_ref[...] / norm
    at_out[...] = a_ref[lax.axis_index("ja")] / na_ref[...]


def add_kernel(*refs):
    parts = [r[...] for r in refs[:-1]]
    while len(parts) > 1:
        parts = [parts[i] + parts[i + 1] for i in range(0, len(parts), 2)]
    refs[-1][...] = parts[0]


def contract(stored_refs, scaled, depth, keep_ref, send_ref):
    group = depth // len(stored_refs)
    core, _ = place()
    columns = [jnp.broadcast_to(scaled[:, k : k + 1], keep_ref.shape[1:]) for k in range(depth)]

    @pl.loop(0, keep_ref.shape[0])
    def _(z):
        for out, which in ((keep_ref, core), (send_ref, 1 - core)):
            out[z] = sum_tree([
                stored_refs[k // group][k % group, 2 * z + which] * columns[k] for k in range(depth)
            ])


def sum_tree(parts):
    while len(parts) > 1:
        parts = [parts[i] + parts[i + 1] for i in range(0, len(parts), 2)]
    return parts[0]


def contract_start_kernel(depth, ct_ref, *refs):
    contract(refs[:GROUPS], ct_ref[...], depth, *refs[GROUPS:])


def contract_kernel(depth, x_ref, y_ref, ga_ref, na_ref, *refs):
    ct_out, gb_out, gc_out, keep_ref, send_ref, inv_ref = refs[GROUPS:]
    ct, gram_b, norm = third_factor(depth, x_ref, y_ref, ga_ref, na_ref, inv_ref)
    ct_out[...] = ct
    gb_out[...] = gram_b
    gc_out[...] = dot(ct, ct, ((1,), (1,)))
    contract(refs[:GROUPS], ct / norm, depth, keep_ref, send_ref)


def spread_kernel(keep_ref, recv_ref, own_ref, *send_refs):
    _, z = place()
    for d, out in enumerate((own_ref,) + send_refs):
        out[...] = keep_ref[z ^ d] + recv_ref[z ^ d]


def gather_kernel(*refs):
    parts, out = refs[:-1], refs[-1]
    _, z = place()
    for d, part in enumerate(parts):
        out[z ^ d] = part[...]


def times_t(w, t):
    return lax.dot_general(w, t, (((1,), (1,)), ((), ())), preferred_element_type=F32)


def load_kernel(group, *refs):
    (t_ref, w_ref, w8_ref, scale_ref), refs = refs[:4], refs[4 if group == 0 else 7 :]
    high_ref, low_ref, unit_ref, stored_ref, ring, sems = refs if group == 0 else refs[1:4] + refs[:1] + refs[4:]
    size, count, _, chunk = stored_ref.shape
    columns = t_ref.shape[2]
    slots = ring.shape[0]
    first, steps = group * size * count, size * count
    part = chunk // 2
    piece = min(64, chunk)

    def copies(step):
        k, at = (first + step) // count, (step % count) * chunk
        return [
            pltpu.make_async_copy(
                t_ref.at[k, pl.ds(pl.multiple_of(at + p * part, part), part), :],
                ring.at[step % slots, pl.ds(p * part, part), :],
                sems.at[step % slots, p],
            )
            for p in range(2)
        ]

    for step in range(slots):
        for copy in copies(step):
            copy.start()

    @pl.loop(0, steps)
    def _(step):
        for copy in copies(step):
            copy.wait()
        k, m = (first + step) // count, step % count
        slot, at = step % slots, pl.multiple_of(m * chunk, chunk)

        def convert(i, top):
            here = pl.ds(pl.multiple_of(i * piece, piece), piece)
            t = ring[slot, here, :]
            high_ref[k, pl.ds(pl.multiple_of(at + i * piece, piece), piece), :] = t.astype(BF16)
            return jnp.maximum(top, jnp.max(jnp.abs(t).reshape(piece // 8, 8, columns), axis=0))

        top = lax.fori_loop(0, chunk // piece, convert, jnp.full((8, columns), TINY, F32))
        unit = jnp.full((1, 128), jnp.max(top)) / (TOP * 256.0)
        inverse = (1.0 / unit)[:, :1]
        unit_ref[first + step] = unit
        rows = pl.ds(at, chunk)
        high = halves(times_t(w_ref[...], high_ref[k, rows, :]))

        @pl.loop(0, chunk // piece)
        def _(i):
            here = pl.ds(pl.multiple_of(i * piece, piece), piece)
            t = ring[slot, here, :]
            low_ref[k, pl.ds(pl.multiple_of(at + i * piece, piece), piece), :] = (
                (t - t.astype(BF16).astype(F32)) * inverse
            ).astype(F8)

        @pl.when(step + slots < steps)
        def _():
            for copy in copies(step + slots):
                copy.start()

        low = halves(times_t(w8_ref[...], low_ref[k, rows, :]) * (scale_ref[...] * unit[:, :1]))
        stored_ref[step // count, m] = high + low


def pass_b_kernel(first, high_ref, low_ref, unit_ref, w_ref, w8_ref, scale_ref, _, stored_ref):
    size, count, _, chunk = stored_ref.shape
    together = max(1, min(count, 512 // chunk))

    @pl.loop(0, size * count // together)
    def _(step):
        i, start = step // (count // together), (step % (count // together)) * together
        k = first + i
        rows = pl.ds(pl.multiple_of(start * chunk, chunk * together), chunk * together)
        high = halves(times_t(w_ref[...], high_ref[k, rows, :]))
        low = times_t(w8_ref[...], low_ref[k, rows, :])
        for n in range(together):
            here = slice(n * chunk, n * chunk + chunk)
            unit = unit_ref[k * count + start + n][:, :1]
            stored_ref[i, start + n] = high[:, here] + halves(low[:, here] * (scale_ref[...] * unit))


def pass_a_kernel(high_ref, low_ref, unit_ref, half_ref, other_ref, inv_ref, ct_ref,
                  a_out, p_out, first_out, second_out, w_ref, w8_ref, acc_ref):
    depth, rows, columns = high_ref.shape
    count, _, chunk = a_out.shape
    core, _ = place()
    products = []
    for z in range(count // 2):
        mine, other = half_ref[z], other_ref[z]
        products += [jnp.where(core == 0, mine, other), jnp.where(core == 0, other, mine)]
    at = dot(inv_ref[...], jnp.concatenate(products, axis=1))
    for m in range(count):
        a_out[m] = at[:, m * chunk : m * chunk + chunk]
    gram = wide(dot(at, at, ((1,), (1,))))
    scale = factor_parts(at, w_ref, w8_ref)
    acc_ref[...] = jnp.zeros_like(acc_ref)

    @pl.loop(0, depth)
    def _(k):
        both = dot16(w_ref[...], high_ref[k])
        for m in range(count):
            here = slice(m * chunk, m * chunk + chunk)
            unit = unit_ref[k * count + m][:, :1]
            both += (scale * unit) * dot16(w8_ref[:, here], low_ref[k, here, :])
        product = halves(both)
        p_out[k] = product
        acc_ref[...] += col_of(ct_ref[...], k) * product

    total = acc_ref[...]
    for out, at in ((first_out, 0), (second_out, 32)):
        out[:, :columns] = total[at : at + 32]
        out[:, columns:] = gram[at : at + 32]


def solve_b_kernel(share, a0_ref, a1_ref, b0_ref, b1_ref, gc_ref, p_ref,
                   bt_out, sums_out, ga_out, na_out, w_out, w8_out, scale_out, inv_ref):
    total = jnp.concatenate([a0_ref[...] + a1_ref[...], b0_ref[...] + b1_ref[...]], axis=0)
    columns = bt_out.shape[1]
    raw = total[:, columns : columns + 64]
    row, col = column_norms(raw)
    gram_a = raw / (row * col)
    invert_into(inv_ref, gram_a * gc_ref[...])
    bt = dot(inv_ref[...], total[:, :columns] / col)
    bt_out[...] = bt
    sums = wide(dot(bt, bt, ((1,), (1,)))) * share
    lane = iota(64, 128, 1)
    for k in range(p_ref.shape[0]):
        sums = jnp.where(lane == 64 + k, jnp.sum(bt * p_ref[k], axis=1, keepdims=True), sums)
    sums_out[...] = sums
    ga_out[...] = gram_a
    na_out[...] = col
    scale_out[...] = factor_parts(bt, w_out, w8_out)


def call(kernel, outs, *operands, scratch=(), mib=1, name=None, flops=200000, nbytes=200000, first=VMEM, keep=(), written=()):
    going = [operands[i] for i in keep + written]
    results, held = len(outs), len(keep)

    def run(*refs):
        rest = refs[len(operands) :]
        kernel(*refs[: len(operands)], *rest[:results], *rest[results + held :])

    return pl.pallas_call(
        run,
        in_specs=[first] + [VMEM] * (len(operands) - 1),
        out_specs=[VMEM] * (results + len(going)),
        out_shape=outs + [held_shape(*x.shape, dtype=x.dtype) for x in going],
        scratch_shapes=scratch,
        input_output_aliases={i: results + n for n, i in enumerate(keep + written)},
        compiler_params=params(mib),
        cost_estimate=cost(flops, nbytes),
        name=name,
    )(*operands)


def held_shape(*dims, dtype=F32):
    return pltpu.VMEM(dims, dtype)


def resident(x):
    return pltpu.with_memory_space_constraint(x, pltpu.VMEM)


def add(*parts):
    return call(add_kernel, [shape(*parts[0].shape)], *parts, name="add")[0]


def inverse_space():
    return [pltpu.VMEM((64, 64), F32)]


def part_shapes(columns):
    return [shape(128, columns, dtype=BF16), shape(128, columns, dtype=F8), shape(128, 1)]


def load(tensor, parts, count, gram):
    steps = masks("ja")
    depth, rows, columns = tensor.shape
    chunk = rows // count
    kept = []
    stored = []
    for g in range(GROUPS):
        new = [] if kept else [
            held_shape(depth, rows, columns, dtype=BF16),
            held_shape(depth, rows, columns, dtype=F8),
            held_shape(depth * count, 1, 128),
        ]
        outs = call(
            functools.partial(load_kernel, g),
            new + [held_shape(depth // GROUPS, count, 64, chunk)],
            tensor, *parts, *[resident(x) for x in kept],
            first=pl.BlockSpec(memory_space=pl.ANY),
            scratch=[
                pltpu.VMEM((SLOTS, chunk, columns), F32), pltpu.SemaphoreType.DMA((SLOTS, 2)),
            ],
            mib=SPACE, name="load", flops=6 * tensor.size * 64 // GROUPS, nbytes=4 * tensor.size // GROUPS,
            written=(4, 5, 6) if kept else (),
        )
        if kept:
            stored.append(outs[0])
            kept = outs[1:]
        else:
            kept, stored = outs[:3], [outs[3]]
        if len(steps) > 1:
            gram = add(gram, across(gram, *steps.pop(0)))
            parts[2], gram = lax.optimization_barrier((parts[2], gram))
    return kept, stored, butterfly(gram, steps)


def pass_a(kept, half, other, inv, ct):
    depth, rows, columns = kept[0].shape
    count, chunk = 2 * half.shape[0], half.shape[2]
    *outs, high, low, unit = call(
        pass_a_kernel,
        [shape(count, 64, chunk), held_shape(depth, 64, columns)] + [shape(32, columns + 128)] * 2,
        *[resident(x) for x in kept], half, other, inv, ct,
        scratch=[
            pltpu.VMEM((128, rows), BF16), pltpu.VMEM((128, rows), F8), pltpu.VMEM((64, columns), F32),
        ],
        mib=SPACE, name="pass_a", flops=6 * kept[0].size * 64, nbytes=3 * kept[0].size, keep=(0, 1, 2),
    )
    return outs, [high, low, unit]


def pass_b(kept, stored, parts):
    size = kept[0].size // GROUPS
    results = []
    for g, old in enumerate(stored):
        *kept, new = call(
            functools.partial(pass_b_kernel, g * old.shape[0]), [],
            *[resident(x) for x in kept], *parts, resident(old),
            mib=SPACE, name="pass_b", flops=6 * size * 64, nbytes=3 * size, keep=(0, 1, 2), written=(6,),
        )
        results.append(new)
    return kept, results


def across(x, axis, mask):
    n = lax.axis_size(axis)
    return lax.ppermute(x, axis, [(i, i ^ mask) for i in range(n)])


def masks(axis):
    return [(axis, 1 << b) for b in range(lax.axis_size(axis).bit_length() - 1)]


def butterfly(x, steps):
    for axis, mask in steps[:-1]:
        x = add(x, across(x, axis, mask))
    axis, mask = steps[-1]
    return x, across(x, axis, mask)


def body(tensor, b_init, c_init):
    depth, rows, columns = tensor.shape
    n_ia, n_ja = lax.axis_size("ia"), lax.axis_size("ja")
    n_z = n_ja // 2
    chunk = rows // n_ja
    everyone = masks("ja") + masks("ia")

    def sum_over_ja(keep, send, grams):
        recv = across(send, "ja", 1)
        if len(grams) == 2:
            (inv,) = call(inverse_kernel, [shape(64, 64)], *grams, name="inverse")
            keep, inv = lax.optimization_barrier((keep, inv))
        own, *sends = call(spread_kernel, [shape(64, chunk)] * n_z, keep, recv, name="spread")
        own = add(own, *[across(s, "ja", 2 * d) for d, s in enumerate(sends, 1)])
        parts = [own] + [across(own, "ja", 2 * d) for d in range(1, n_z)]
        (mine,) = call(gather_kernel, [shape(n_z, 64, chunk)], *parts, name="gather")
        if len(grams) == 3:
            _, inv = call(first_inverse_kernel, [shape(64, 64)] * 2, *grams, name="inverse")
        return mine, across(mine, "ja", 1), inv

    def sum_over_ia(first, second):
        order = masks("ia")
        return butterfly(first, order) + butterfly(second, order[1:] + order[:1])

    gram, ct, gram_c, *parts = call(
        start_kernel,
        [shape(64, 128), shape(64, 128), shape(64, 64)] + part_shapes(columns),
        b_init.T, c_init, name="start",
    )
    kept, stored, grams = load(tensor, parts, n_ja, gram)
    grams = grams + (gram_c,)
    keep, send = call(
        functools.partial(contract_start_kernel, depth), [shape(n_z, 64, chunk)] * 2,
        ct, *[resident(x) for x in stored],
        name="contract", flops=tensor.size // 8, nbytes=tensor.size // 4,
    )
    for sweep in range(SWEEPS):
        last = sweep == SWEEPS - 1
        mine, other, inv = sum_over_ja(keep, send, grams)
        (a, products, first, second), kept = pass_a(kept, mine, other, inv, ct)
        bt, sums, gram_a, norm_a, *parts = call(
            functools.partial(solve_b_kernel, 1.0 / n_ia),
            [shape(64, columns), shape(64, 128), shape(64, 64), shape(64, 1)] + part_shapes(columns),
            *sum_over_ia(first, second), gram_c, products, scratch=inverse_space(), mib=SOLVE, name="solve_b",
        )
        sums = butterfly(sums, everyone)
        if last:
            break
        kept, stored = pass_b(kept, stored, parts)
        ct, gram_b, gram_c, keep, send = call(
            functools.partial(contract_kernel, depth),
            [shape(64, 128), shape(64, 64), shape(64, 64)] + [shape(n_z, 64, chunk)] * 2,
            *sums, gram_a, norm_a, *[resident(x) for x in stored], scratch=inverse_space(),
            name="contract", flops=tensor.size // 8, nbytes=tensor.size // 4,
        )
        grams = (gram_b, gram_c)
    ct, bt, at = call(
        last_kernel, [shape(64, depth), shape(64, columns), shape(64, chunk)],
        *sums, gram_a, norm_a, bt, a, scratch=inverse_space(), mib=3, name="last",
    )
    return at.T, bt.T, ct.T


def solution(mesh):
    in_specs = (P(None, "ia", "ja"), P("ja", None), P())
    out_specs = (P(("ia", "ja"), None), P("ja", None), P())
    return jax.shard_map(body, mesh=mesh, in_specs=in_specs, out_specs=out_specs, check_vma=False)
```

```python
import functools

import jax
import jax.numpy as jnp
from jax import lax
from jax.experimental import pallas as pl
from jax.experimental.pallas import tpu as pltpu
from jax.sharding import PartitionSpec as P

SWEEPS = 4
EPS = 1e-6
HIGH = lax.Precision.HIGHEST
F32 = jnp.float32
BF16 = jnp.bfloat16
F8 = jnp.float8_e4m3fn
TOP = 224.0
TINY = 1e-30
GROUPS = 4
CHUNK = 1024
SPACE = 6
SMALL = 1
VMEM = pl.BlockSpec(memory_space=pltpu.VMEM)
MIB = 1 << 20


def params(mib):
    return pltpu.CompilerParams(vmem_limit_bytes=int(mib * MIB))


def cost(flops, nbytes):
    return pl.CostEstimate(flops=int(flops), bytes_accessed=int(nbytes), transcendentals=0)


def shape(*dims, dtype=F32):
    return jax.ShapeDtypeStruct(dims, dtype)


def dot(a, b, dims=((1,), (0,))):
    return lax.dot_general(a, b, (dims, ((), ())), precision=HIGH, preferred_element_type=F32)


def dot16(a, b):
    return jnp.dot(a, b, preferred_element_type=F32)


def split(x):
    hi = x.astype(BF16)
    return hi, (x - hi.astype(F32)).astype(BF16)


def iota(rows, cols, dim):
    return lax.broadcasted_iota(jnp.int32, (rows, cols), dim)


def eye(n):
    return (iota(n, n, 0) == iota(n, n, 1)).astype(F32)


def column_norms(raw):
    diagonal = raw * eye(raw.shape[0])
    row = jnp.sqrt(jnp.sum(diagonal, axis=0, keepdims=True) + EPS)
    col = jnp.sqrt(jnp.sum(diagonal, axis=1, keepdims=True) + EPS)
    return row, col


def eliminate(g):
    n = g.shape[0]
    m = jnp.concatenate([g, eye(n)], axis=1)
    rows = iota(n, 2 * n, 0)
    for k in range(n):
        pivot = m[k : k + 1, :] / m[k : k + 1, k : k + 1]
        m = jnp.where(rows == k, pivot, m - m[:, k : k + 1] * pivot)
    return m[:, n:]


def invert_into(out_ref, g):
    n = g.shape[0]
    one = eye(n)
    diagonal = g * one
    row = lax.rsqrt(jnp.sum(diagonal, axis=0, keepdims=True))
    col = lax.rsqrt(jnp.sum(diagonal, axis=1, keepdims=True))
    power = one - g * (row * col)
    close = jnp.sum(power * power) <= 0.25

    @pl.when(close)
    def _():
        e = power
        total = one + e
        for _ in range(4):
            e = dot(e, e)
            total = total + dot(total, e)
        out_ref[...] = total * (row * col)

    @pl.when(jnp.logical_not(close))
    def _():
        out_ref[...] = eliminate(g)


def block_diagonal(g):
    zero = jnp.zeros_like(g)
    return jnp.concatenate(
        [jnp.concatenate([g, zero], axis=1), jnp.concatenate([zero, g], axis=1)], axis=0
    )


def wide(x):
    return jnp.concatenate([x, x], axis=1)


def row_of(col):
    return jnp.sum(eye(col.shape[0]) * col, axis=0, keepdims=True)


def col_of(row):
    return jnp.sum(eye(row.shape[1]) * row, axis=1, keepdims=True)


def split8(x, unit):
    x = x / unit
    hi = x.astype(F8).astype(F32)
    return hi, ((x - hi) * 16.0).astype(F8).astype(F32)


def start_kernel(bt_ref, c_ref, gb_ref, c_out, gc_ref):
    bt = bt_ref[...]
    gb_ref[...] = wide(dot(bt, bt, ((1,), (1,))))
    c = c_ref[...]
    c_out[...] = wide(c)
    gc_ref[...] = dot(c, c, ((0,), (0,)))


def first_inverse_kernel(x_ref, y_ref, gc_ref, gb_out, inv_out, inv_ref):
    gram_b = x_ref[:, :64] + y_ref[:, :64]
    gb_out[...] = gram_b
    invert_into(inv_ref, gram_b * gc_ref[...])
    inv_out[...] = block_diagonal(inv_ref[...])


def inverse_kernel(x_ref, y_ref, out_ref, inv_ref):
    invert_into(inv_ref, x_ref[...] * y_ref[...])
    out_ref[...] = block_diagonal(inv_ref[...])


def third_factor(depth, x_ref, y_ref, ga_ref, na_ref, inv_ref):
    total = x_ref[...] + y_ref[...]
    raw = total[:, :64]
    row, col = column_norms(raw)
    gram_b = raw / (row * col)
    invert_into(inv_ref, gram_b * ga_ref[...])
    three = total.T[64 : 64 + depth, :] / (na_ref[...] * row)
    return dot(three, inv_ref[...]), gram_b, row, col


def last_kernel(x_ref, y_ref, ga_ref, na_ref, bt_ref, a_ref, c_out, b_out, a_out, inv_ref):
    c, _, _, col = third_factor(c_out.shape[0], x_ref, y_ref, ga_ref, na_ref, inv_ref)
    c_out[...] = c
    b_out[...] = bt_ref[...] / col
    a_out[...] = a_ref[...] / wide(na_ref[...])


def place():
    ja = lax.axis_index("ja")
    return lax.rem(ja, 2), lax.div(ja, 2)


def add_kernel(*refs):
    parts = [r[...] for r in refs[:-1]]
    while len(parts) > 1:
        parts = [parts[i] + parts[i + 1] for i in range(0, len(parts), 2)]
    refs[-1][...] = parts[0]


def contract(stored_refs, scaled, keep_ref, send_ref):
    depth = scaled.shape[0]
    group = depth // len(stored_refs)
    part = stored_refs[0].shape[1] // 2
    chunk = min(64, part)
    core, _ = place()
    for out, which in ((keep_ref, core), (send_ref, 1 - core)):

        @pl.loop(0, part // chunk)
        def _(i):
            at = pl.multiple_of(which * part + i * chunk, chunk)
            total = None
            for k in range(depth):
                term = stored_refs[k // group][k % group, pl.ds(at, chunk), :] * scaled[k : k + 1, :]
                total = term if total is None else total + term
            out[pl.ds(pl.multiple_of(i * chunk, chunk), chunk), :] = total


def contract_start_kernel(c_ref, *refs):
    contract(refs[:GROUPS], c_ref[...], *refs[GROUPS:])


def contract_kernel(x_ref, y_ref, ga_ref, na_ref, *refs):
    c_out, gb_out, gc_out, keep_ref, send_ref, inv_ref = refs[GROUPS:]
    c, gram_b, norm, _ = third_factor(c_out.shape[0], x_ref, y_ref, ga_ref, na_ref, inv_ref)
    c_out[...] = wide(c)
    gb_out[...] = gram_b
    gc_out[...] = dot(c, c, ((0,), (0,)))
    contract(refs[:GROUPS], wide(c / norm), keep_ref, send_ref)


def spread_kernel(keep_ref, recv_ref, own_ref, *send_refs):
    rows = own_ref.shape[0]
    _, z = place()
    for d, out in enumerate((own_ref,) + send_refs):
        at = pl.multiple_of((z ^ d) * rows, rows)
        out[...] = keep_ref[pl.ds(at, rows), :] + recv_ref[pl.ds(at, rows), :]


def gather_kernel(*refs):
    parts, out = refs[:-1], refs[-1]
    rows = parts[0].shape[0]
    _, z = place()
    for d, part in enumerate(parts):
        at = pl.multiple_of((z ^ d) * rows, rows)
        out[pl.ds(at, rows), :] = part[...]


def second_weights(bt_ref, w_ref, w8_ref):
    unit = jnp.maximum(jnp.max(jnp.abs(bt_ref[...]), axis=1, keepdims=True), TINY) / TOP
    columns = bt_ref.shape[1]
    chunk = min(128, columns)

    @pl.loop(0, columns // chunk)
    def _(i):
        here = pl.ds(pl.multiple_of(i * chunk, chunk), chunk)
        part = bt_ref[:, here]
        hi = part.astype(BF16).astype(F32)
        for out, parts in ((w_ref, (hi, part - hi)), (w8_ref, split8(part, unit))):
            b = jnp.concatenate(parts, axis=0).T
            turned = pltpu.roll(b, 64, 1)
            out[0, here, :] = b.astype(out.dtype)
            out[1, here, :] = turned.astype(out.dtype)

    return wide(row_of(unit))


def times_b(first, second, weights):
    x, y = dot16(first, weights[0]), dot16(second, weights[1])
    left = iota(*x.shape, 1) < 64
    return jnp.where(left, x, y), pltpu.roll(jnp.where(left, y, x), 64, 1)


def times_both(high0, high1, low0, low1, w_ref, w8_ref):
    high, high_rest = times_b(high0, high1, w_ref)
    low, low_rest = times_b(low0, low1, w8_ref)
    return high + high_rest, low + low_rest * 0.0625


def load_kernel(group, *refs):
    (t_ref, w_ref, w8_ref, scale_ref), refs = refs[:4], refs[4 if group == 0 else 7 :]
    high_ref, low_ref, unit_ref, stored_ref, ring, sems = refs if group == 0 else refs[1:4] + refs[:1] + refs[4:]
    size, half, _ = stored_ref.shape
    columns = t_ref.shape[3]
    slots, _, block, _ = ring.shape
    count = half // block
    first, steps = group * size * count, size * count
    piece, small = min(64, block), min(32, block)

    def copies(step):
        k, at = (first + step) // count, pl.multiple_of((step % count) * block, block)
        return [
            pltpu.make_async_copy(
                t_ref.at[k, h, pl.ds(at, block), :], ring.at[step % slots, h], sems.at[step % slots, h]
            )
            for h in range(2)
        ]

    for step in range(slots):
        for copy in copies(step):
            copy.start()

    @pl.loop(0, steps)
    def _(step):
        for copy in copies(step):
            copy.wait()
        k, at = (first + step) // count, pl.multiple_of((step % count) * block, block)
        slot = step % slots
        rows = pl.ds(at, block)

        def convert(i, top):
            here = pl.ds(pl.multiple_of(i * piece, piece), piece)
            there = pl.ds(pl.multiple_of(at + i * piece, piece), piece)
            for h in range(2):
                hi = ring[slot, h, here, :].astype(BF16)
                high_ref[k, h, there, :] = hi
                top = jnp.maximum(top, jnp.max(jnp.abs(hi).reshape(piece // 16, 16, columns), axis=0))
            return top

        top = lax.fori_loop(0, block // piece, convert, jnp.full((16, columns), TINY, BF16))
        inverse = ((TOP * 256.0) / jnp.full((1, 128), jnp.max(top.astype(F32)))).astype(BF16)
        unit = 1.0 / inverse.astype(F32)
        unit_ref[first + step] = unit
        high, rest = times_b(high_ref[k, 0, rows, :], high_ref[k, 1, rows, :], w_ref)
        high = high + rest
        for i in range(block // small):
            there = pl.ds(pl.multiple_of(at + i * small, small), small)
            for h in range(2):
                hi = high_ref[k, h, there, :].astype(F32)
                lo = (ring[slot, h, i * small : i * small + small, :] - hi).astype(BF16)
                low_ref[k, h, there, :] = (lo * inverse[:, :1]).astype(F8)

        @pl.when(step + slots < steps)
        def _():
            for copy in copies(step + slots):
                copy.start()

        low, rest = times_b(low_ref[k, 0, rows, :], low_ref[k, 1, rows, :], w8_ref)
        stored_ref[step // count, rows, :] = high + (low + rest * 0.0625) * (scale_ref[...] * unit)


def weights_kernel(bt_ref, w_ref, w8_ref, scale_ref):
    scale_ref[...] = second_weights(bt_ref, w_ref, w8_ref)


def pass_b_kernel(first, depth, high_ref, low_ref, unit_ref, w_ref, w8_ref, scale_ref, _, stored_ref):
    half = high_ref.shape[2]
    count = unit_ref.shape[0] // depth
    block = half // count
    chunk = min(CHUNK, half)

    @pl.loop(0, stored_ref.shape[0])
    def _(i):
        k = first + i
        for q in range(0, half, chunk):
            rows = slice(q, q + chunk)
            high, low = times_both(
                high_ref[k, 0, rows, :], high_ref[k, 1, rows, :],
                low_ref[k, 0, rows, :], low_ref[k, 1, rows, :], w_ref, w8_ref,
            )
            for at in range(0, chunk, block):
                here = slice(at, at + block)
                unit = unit_ref[k * count + (q + at) // block]
                stored_ref[i, q + at : q + at + block, :] = high[here] + low[here] * (scale_ref[...] * unit)


def pass_a_kernel(high_ref, low_ref, unit_ref, half_ref, other_ref, inv_ref, c_ref,
                  a_out, p_out, first_out, second_out, w_ref, w8_ref, acc_ref):
    depth, _, half, columns = high_ref.shape
    count = unit_ref.shape[0] // depth
    block = half // count
    part = half // 2
    core, _ = place()
    inv = inv_ref[...]
    a_out[pl.ds(pl.multiple_of(core * part, part), part), :] = dot(half_ref[...], inv)
    a_out[pl.ds(pl.multiple_of((1 - core) * part, part), part), :] = dot(other_ref[...], inv)
    at = a_out[...].T
    gram = dot(at, at, ((1,), (1,)))
    gram = wide(gram[:64, :64] + gram[64:, 64:])
    top = jnp.max(jnp.abs(at), axis=1, keepdims=True)
    unit = jnp.maximum(jnp.maximum(top[:64], top[64:]), TINY) / TOP
    for h in range(2):
        rows = at[64 * h : 64 * h + 64]
        hi, lo = split(rows)
        w_ref[h, :64, :] = hi
        w_ref[h, 64:, :] = lo
        hi8, lo8 = split8(rows, unit)
        w8_ref[h, :64, :] = hi8.astype(F8)
        w8_ref[h, 64:, :] = lo8.astype(F8)
    units = jnp.concatenate([unit, unit * 0.0625], axis=0)
    acc_ref[...] = jnp.zeros_like(acc_ref)

    @pl.loop(0, depth)
    def _(k):
        row = jnp.sum(jnp.where(iota(depth, 128, 0) == k, c_ref[...], 0.0), axis=0, keepdims=True)
        col = col_of(row[:, :64])
        both = dot16(w_ref[0], high_ref[k, 0]) + dot16(w_ref[1], high_ref[k, 1])
        for b in range(count):
            rows = slice(b * block, b * block + block)
            low = dot16(w8_ref[0, :, rows], low_ref[k, 0, rows, :])
            low += dot16(w8_ref[1, :, rows], low_ref[k, 1, rows, :])
            both += (units * unit_ref[k * count + b][:, :1]) * low
        product = both[:64] + both[64:]
        p_out[k] = product
        acc_ref[...] += col * product

    total = acc_ref[...]
    first_out[:, :columns] = total[:32]
    second_out[:, :columns] = total[32:]
    first_out[:, columns:] = gram[:32]
    second_out[:, columns:] = gram[32:]


def solve_b_kernel(share, a0_ref, a1_ref, b0_ref, b1_ref, gc_ref, p_ref, bt_out, sums_out, ga_out, na_out, inv_ref):
    total = jnp.concatenate([a0_ref[...] + a1_ref[...], b0_ref[...] + b1_ref[...]], axis=0)
    columns = bt_out.shape[1]
    raw = total[:, columns : columns + 64]
    row, col = column_norms(raw)
    gram_a = raw / (row * col)
    invert_into(inv_ref, gram_a * gc_ref[...])
    bt = dot(inv_ref[...], total[:, :columns] / col)
    bt_out[...] = bt
    sums = wide(dot(bt, bt, ((1,), (1,)))) * share
    lane = iota(64, 128, 1)
    for k in range(p_ref.shape[0]):
        sums = jnp.where(lane == 64 + k, jnp.sum(bt * p_ref[k], axis=1, keepdims=True), sums)
    sums_out[...] = sums
    ga_out[...] = gram_a
    na_out[...] = row


def call(kernel, outs, *operands, scratch=(), mib=SMALL, name=None, flops=200000, nbytes=200000, first=VMEM, keep=(), written=()):
    going = [operands[i] for i in keep + written]
    results, held = len(outs), len(keep)

    def run(*refs):
        rest = refs[len(operands) :]
        kernel(*refs[: len(operands)], *rest[:results], *rest[results + held :])

    return pl.pallas_call(
        run,
        in_specs=[first] + [VMEM] * (len(operands) - 1),
        out_specs=[VMEM] * (results + len(going)),
        out_shape=outs + [pltpu.VMEM(x.shape, x.dtype) for x in going],
        scratch_shapes=scratch,
        input_output_aliases={i: results + n for n, i in enumerate(keep + written)},
        compiler_params=params(mib),
        cost_estimate=cost(flops, nbytes),
        name=name,
    )(*operands)


def resident(x):
    return pltpu.with_memory_space_constraint(x, pltpu.VMEM)


def add(*parts):
    return call(add_kernel, [shape(*parts[0].shape)], *parts, name="add")[0]


def inverse_space():
    return [pltpu.VMEM((64, 64), F32)]


def make_weights(bt):
    columns = bt.shape[1]
    return call(
        weights_kernel,
        [shape(2, columns, 128, dtype=BF16), shape(2, columns, 128, dtype=F8), shape(1, 128)],
        bt, name="weights",
    )


def load(tensor, bt, gram):
    depth, rows, columns = tensor.shape
    half = rows // 2
    block = min(256, half)
    weights, steps = list(make_weights(bt)), masks("ja")
    kept, stored = [], []
    for g in range(GROUPS):
        new = [] if kept else [
            pltpu.VMEM((depth, 2, half, columns), BF16),
            pltpu.VMEM((depth, 2, half, columns), F8),
            pltpu.VMEM((depth * (half // block), 1, 128), F32),
        ]
        outs = call(
            functools.partial(load_kernel, g),
            new + [pltpu.VMEM((depth // GROUPS, half, 128), F32)],
            tensor.reshape(depth, 2, half, columns), *weights, *[resident(x) for x in kept],
            first=pl.BlockSpec(memory_space=pl.ANY),
            scratch=[
                pltpu.VMEM((2, 2, block, columns), F32), pltpu.SemaphoreType.DMA((2, 2)),
            ],
            mib=SPACE, name="load", flops=6 * tensor.size * 64 // GROUPS, nbytes=4 * tensor.size // GROUPS,
            written=(4, 5, 6) if kept else (),
        )
        if kept:
            stored.append(outs[0])
            kept = outs[1:]
        else:
            kept, stored = outs[:3], [outs[3]]
        if len(steps) > 1:
            gram = add(gram, across(gram, *steps.pop(0)))
            weights[2], gram = lax.optimization_barrier((weights[2], gram))
    return kept, stored, butterfly(gram, steps)


def pass_a(kept, half, other, inv, c):
    depth, _, rows, columns = kept[0].shape
    *outs, high, low, unit = call(
        pass_a_kernel,
        [shape(rows, 128), pltpu.VMEM((depth, 64, columns), F32)] + [shape(32, columns + 128)] * 2,
        *[resident(x) for x in kept], half, other, inv, c,
        scratch=[
            pltpu.VMEM((2, 128, rows), BF16), pltpu.VMEM((2, 128, rows), F8),
            pltpu.VMEM((64, columns), F32),
        ],
        mib=SPACE, name="pass_a", flops=6 * kept[0].size * 64, nbytes=3 * kept[0].size, keep=(0, 1, 2),
    )
    return outs, [high, low, unit]


def pass_b(kept, stored, bt):
    weights = make_weights(bt)
    size = kept[0].size // GROUPS
    results = []
    for g, old in enumerate(stored):
        *kept, new = call(
            functools.partial(pass_b_kernel, g * old.shape[0], kept[0].shape[0]), [],
            *[resident(x) for x in kept], *weights, resident(old),
            mib=SPACE, name="pass_b", flops=6 * size * 64, nbytes=3 * size, keep=(0, 1, 2), written=(6,),
        )
        results.append(new)
    return kept, results


def across(x, axis, mask):
    n = lax.axis_size(axis)
    return lax.ppermute(x, axis, [(i, i ^ mask) for i in range(n)])


def masks(axis):
    return [(axis, 1 << b) for b in range(lax.axis_size(axis).bit_length() - 1)]


def butterfly(x, steps):
    for axis, mask in steps[:-1]:
        x = add(x, across(x, axis, mask))
    axis, mask = steps[-1]
    return x, across(x, axis, mask)


def body(tensor, b_init, c_init):
    depth, rows, columns = tensor.shape
    half = rows // 2
    n_ia, n_ja = lax.axis_size("ia"), lax.axis_size("ja")
    n_z = n_ja // 2
    ja = lax.axis_index("ja")
    piece = half // 2 // n_z

    everyone = masks("ja") + masks("ia")
    bt = b_init.T
    gram, c, gram_c = call(
        start_kernel, [shape(64, 128), shape(depth, 128), shape(64, 64)], bt, c_init, name="start",
    )
    kept, stored, grams = load(tensor, bt, gram)

    def sum_over_ja(keep, send, grams):
        recv = across(send, "ja", 1)
        if len(grams) == 2:
            (inv,) = call(inverse_kernel, [shape(128, 128)], *grams, scratch=inverse_space(), name="inverse")
            keep, inv = lax.optimization_barrier((keep, inv))
        own, *sends = call(
            spread_kernel, [shape(piece, 128)] * n_z, keep, recv, name="spread"
        )
        own = add(own, *[across(s, "ja", 2 * d) for d, s in enumerate(sends, 1)])
        parts = [own] + [across(own, "ja", 2 * d) for d in range(1, n_z)]
        (mine,) = call(gather_kernel, [shape(half // 2, 128)], *parts, name="gather")
        gram_b = None
        if len(grams) == 3:
            gram_b, inv = call(
                first_inverse_kernel, [shape(64, 64), shape(128, 128)], *grams,
                scratch=inverse_space(), name="inverse",
            )
        return mine, across(mine, "ja", 1), inv

    def sum_over_ia(first, second):
        order = masks("ia")
        return butterfly(first, order) + butterfly(second, order[1:] + order[:1])

    keep, send = call(
        contract_start_kernel, [shape(half // 2, 128)] * 2, c, *[resident(x) for x in stored],
        name="contract", flops=tensor.size // 8, nbytes=tensor.size // 4,
    )
    grams = grams + (gram_c,)
    for sweep in range(SWEEPS):
        last = sweep == SWEEPS - 1
        mine, other, inv = sum_over_ja(keep, send, grams)
        (a, products, first, second), kept = pass_a(kept, mine, other, inv, c)
        bt, sums, gram_a, norm_a = call(
            functools.partial(solve_b_kernel, 1.0 / n_ia),
            [shape(64, columns), shape(64, 128), shape(64, 64), shape(1, 64)],
            *sum_over_ia(first, second), gram_c, products, scratch=inverse_space(), mib=3, name="solve_b",
        )
        sums = butterfly(sums, everyone)
        if last:
            break
        kept, stored = pass_b(kept, stored, bt)
        c, gram_b, gram_c, keep, send = call(
            contract_kernel,
            [shape(depth, 128), shape(64, 64), shape(64, 64)] + [shape(half // 2, 128)] * 2,
            *sums, gram_a, norm_a, *[resident(x) for x in stored], scratch=inverse_space(),
            name="contract", flops=tensor.size // 8, nbytes=tensor.size // 4,
        )
        grams = (gram_b, gram_c)
    factor_c, bt, a = call(
        last_kernel, [shape(depth, 64), shape(64, columns), shape(half, 128)],
        *sums, gram_a, norm_a, bt, a, scratch=inverse_space(), mib=3, name="last",
    )
    share = rows // n_ja
    at = ja * share
    mine = lax.dynamic_slice_in_dim(a, at % half, share, 0)
    factor_a = jnp.where(at < half, mine[:, :64], mine[:, 64:])
    return factor_a, bt.T, factor_c


def solution(mesh):
    in_specs = (P(None, "ia", "ja"), P("ja", None), P())
    out_specs = (P(("ia", "ja"), None), P("ja", None), P())
    return jax.shard_map(body, mesh=mesh, in_specs=in_specs, out_specs=out_specs, check_vma=False)
```

```python
import functools

import jax
import jax.numpy as jnp
from jax import lax
from jax.experimental import pallas as pl
from jax.experimental.pallas import tpu as pltpu
from jax.sharding import PartitionSpec as P

SWEEPS = 4
EPS = 1e-6
HIGH = lax.Precision.HIGHEST
F32 = jnp.float32
BF16 = jnp.bfloat16
F8 = jnp.float8_e4m3fn
TOP = 224.0
TINY = 1e-30
GROUPS = 4
CHUNK = 1024
SPACE = 6.25
SMALL = 1
VMEM = pl.BlockSpec(memory_space=pltpu.VMEM)
MIB = 1 << 20


def params(mib):
    return pltpu.CompilerParams(vmem_limit_bytes=int(mib * MIB))


def cost(flops, nbytes):
    return pl.CostEstimate(flops=int(flops), bytes_accessed=int(nbytes), transcendentals=0)


def shape(*dims, dtype=F32):
    return jax.ShapeDtypeStruct(dims, dtype)


def dot(a, b, dims=((1,), (0,))):
    return lax.dot_general(a, b, (dims, ((), ())), precision=HIGH, preferred_element_type=F32)


def dot16(a, b):
    return jnp.dot(a, b, preferred_element_type=F32)


def split(x):
    hi = x.astype(BF16)
    return hi, (x - hi.astype(F32)).astype(BF16)


def iota(rows, cols, dim):
    return lax.broadcasted_iota(jnp.int32, (rows, cols), dim)


def eye(n):
    return (iota(n, n, 0) == iota(n, n, 1)).astype(F32)


def column_norms(raw):
    diagonal = raw * eye(raw.shape[0])
    row = jnp.sqrt(jnp.sum(diagonal, axis=0, keepdims=True) + EPS)
    col = jnp.sqrt(jnp.sum(diagonal, axis=1, keepdims=True) + EPS)
    return row, col


def eliminate(g):
    n = g.shape[0]
    m = jnp.concatenate([g, eye(n)], axis=1)
    rows = iota(n, 2 * n, 0)
    for k in range(n):
        pivot = m[k : k + 1, :] / m[k : k + 1, k : k + 1]
        m = jnp.where(rows == k, pivot, m - m[:, k : k + 1] * pivot)
    return m[:, n:]


def invert_into(out_ref, g):
    n = g.shape[0]
    one = eye(n)
    diagonal = g * one
    row = lax.rsqrt(jnp.sum(diagonal, axis=0, keepdims=True))
    col = lax.rsqrt(jnp.sum(diagonal, axis=1, keepdims=True))
    power = one - g * (row * col)
    close = jnp.sum(power * power) <= 0.25

    @pl.when(close)
    def _():
        e = power
        total = one + e
        for _ in range(4):
            e = dot(e, e)
            total = total + dot(total, e)
        out_ref[...] = total * (row * col)

    @pl.when(jnp.logical_not(close))
    def _():
        out_ref[...] = eliminate(g)


def block_diagonal(g):
    zero = jnp.zeros_like(g)
    return jnp.concatenate(
        [jnp.concatenate([g, zero], axis=1), jnp.concatenate([zero, g], axis=1)], axis=0
    )


def wide(x):
    return jnp.concatenate([x, x], axis=1)


def row_of(col):
    return jnp.sum(eye(col.shape[0]) * col, axis=0, keepdims=True)


def col_of(row):
    return jnp.sum(eye(row.shape[1]) * row, axis=1, keepdims=True)


def split8(x, unit):
    x = x / unit
    hi = x.astype(F8).astype(F32)
    return hi, ((x - hi) * 16.0).astype(F8).astype(F32)


def start_kernel(bt_ref, c_ref, gb_ref, c_out, gc_ref):
    bt = bt_ref[...]
    gb_ref[...] = wide(dot(bt, bt, ((1,), (1,))))
    c = c_ref[...]
    c_out[...] = wide(c)
    gc_ref[...] = dot(c, c, ((0,), (0,)))


def first_inverse_kernel(x_ref, y_ref, gc_ref, gb_out, inv_out, inv_ref):
    gram_b = x_ref[:, :64] + y_ref[:, :64]
    gb_out[...] = gram_b
    invert_into(inv_ref, gram_b * gc_ref[...])
    inv_out[...] = block_diagonal(inv_ref[...])


def inverse_kernel(x_ref, y_ref, out_ref, inv_ref):
    invert_into(inv_ref, x_ref[...] * y_ref[...])
    out_ref[...] = block_diagonal(inv_ref[...])


def third_factor(depth, x_ref, y_ref, ga_ref, na_ref, inv_ref):
    total = x_ref[...] + y_ref[...]
    raw = total[:, :64]
    row, col = column_norms(raw)
    gram_b = raw / (row * col)
    invert_into(inv_ref, gram_b * ga_ref[...])
    three = total.T[64 : 64 + depth, :] / (na_ref[...] * row)
    return dot(three, inv_ref[...]), gram_b, row, col


def last_kernel(x_ref, y_ref, ga_ref, na_ref, bt_ref, a_ref, c_out, b_out, a_out, inv_ref):
    c, _, _, col = third_factor(c_out.shape[0], x_ref, y_ref, ga_ref, na_ref, inv_ref)
    c_out[...] = c
    b_out[...] = bt_ref[...] / col
    a_out[...] = a_ref[...] / wide(na_ref[...])


def place():
    ja = lax.axis_index("ja")
    return lax.rem(ja, 2), lax.div(ja, 2)


def add_kernel(*refs):
    parts = [r[...] for r in refs[:-1]]
    while len(parts) > 1:
        parts = [parts[i] + parts[i + 1] for i in range(0, len(parts), 2)]
    refs[-1][...] = parts[0]


def contract(stored_refs, scaled, keep_ref, send_ref):
    depth = scaled.shape[0]
    group = depth // len(stored_refs)
    part = stored_refs[0].shape[1] // 2
    chunk = min(64, part)
    core, _ = place()
    for out, which in ((keep_ref, core), (send_ref, 1 - core)):

        @pl.loop(0, part // chunk)
        def _(i):
            at = pl.multiple_of(which * part + i * chunk, chunk)
            total = None
            for k in range(depth):
                term = stored_refs[k // group][k % group, pl.ds(at, chunk), :] * scaled[k : k + 1, :]
                total = term if total is None else total + term
            out[pl.ds(pl.multiple_of(i * chunk, chunk), chunk), :] = total


def contract_start_kernel(c_ref, *refs):
    contract(refs[:GROUPS], c_ref[...], *refs[GROUPS:])


def contract_kernel(x_ref, y_ref, ga_ref, na_ref, *refs):
    c_out, gb_out, gc_out, keep_ref, send_ref, inv_ref = refs[GROUPS:]
    c, gram_b, norm, _ = third_factor(c_out.shape[0], x_ref, y_ref, ga_ref, na_ref, inv_ref)
    c_out[...] = wide(c)
    gb_out[...] = gram_b
    gc_out[...] = dot(c, c, ((0,), (0,)))
    contract(refs[:GROUPS], wide(c / norm), keep_ref, send_ref)


def spread_kernel(keep_ref, recv_ref, own_ref, *send_refs):
    rows = own_ref.shape[0]
    _, z = place()
    for d, out in enumerate((own_ref,) + send_refs):
        at = pl.multiple_of((z ^ d) * rows, rows)
        out[...] = keep_ref[pl.ds(at, rows), :] + recv_ref[pl.ds(at, rows), :]


def gather_kernel(*refs):
    parts, out = refs[:-1], refs[-1]
    rows = parts[0].shape[0]
    _, z = place()
    for d, part in enumerate(parts):
        at = pl.multiple_of((z ^ d) * rows, rows)
        out[pl.ds(at, rows), :] = part[...]


def second_weights(bt_ref, w_ref, w8_ref):
    unit = jnp.maximum(jnp.max(jnp.abs(bt_ref[...]), axis=1, keepdims=True), TINY) / TOP
    columns = bt_ref.shape[1]
    chunk = min(128, columns)

    @pl.loop(0, columns // chunk)
    def _(i):
        here = pl.ds(pl.multiple_of(i * chunk, chunk), chunk)
        part = bt_ref[:, here]
        hi = part.astype(BF16).astype(F32)
        for out, parts in ((w_ref, (hi, part - hi)), (w8_ref, split8(part, unit))):
            b = jnp.concatenate(parts, axis=0).T
            turned = pltpu.roll(b, 64, 1)
            out[0, here, :] = b.astype(out.dtype)
            out[1, here, :] = turned.astype(out.dtype)

    return wide(row_of(unit))


def times_b(first, second, weights):
    x, y = dot16(first, weights[0]), dot16(second, weights[1])
    left = iota(*x.shape, 1) < 64
    return jnp.where(left, x, y), pltpu.roll(jnp.where(left, y, x), 64, 1)


def times_both(high0, high1, low0, low1, w_ref, w8_ref):
    high, high_rest = times_b(high0, high1, w_ref)
    low, low_rest = times_b(low0, low1, w8_ref)
    return high + high_rest, low + low_rest * 0.0625


def load_kernel(group, *refs):
    (t_ref, w_ref, w8_ref, scale_ref), refs = refs[:4], refs[4 if group == 0 else 7 :]
    high_ref, low_ref, unit_ref, stored_ref, ring, rest_ref, sems = refs if group == 0 else refs[1:4] + refs[:1] + refs[4:]
    size, half, _ = stored_ref.shape
    columns = t_ref.shape[3]
    slots, block, _ = ring.shape
    count = half // block
    first, steps = group * size * count, size * count
    piece, small, part = min(64, block), min(32, block), block // 2

    def copies(turn):
        step, h = turn // 2, turn % 2
        k, at = (first + step) // count, (step % count) * block
        return [
            pltpu.make_async_copy(
                t_ref.at[k, h, pl.ds(pl.multiple_of(at + p * part, part), part), :],
                ring.at[turn % slots, pl.ds(p * part, part), :],
                sems.at[turn % slots, p],
            )
            for p in range(2)
        ]

    for turn in range(slots):
        for copy in copies(turn):
            copy.start()

    @pl.loop(0, steps)
    def _(step):
        k, at = (first + step) // count, pl.multiple_of((step % count) * block, block)
        rows = pl.ds(at, block)
        top = jnp.full((16, columns), TINY, BF16)
        for h in range(2):
            turn = 2 * step + h
            for copy in copies(turn):
                copy.wait()

            def convert(i, top):
                here = pl.ds(pl.multiple_of(i * piece, piece), piece)
                there = pl.ds(pl.multiple_of(at + i * piece, piece), piece)
                t = ring[turn % slots, here, :]
                hi = t.astype(BF16)
                high_ref[k, h, there, :] = hi
                rest_ref[h, here, :] = (t - hi.astype(F32)).astype(BF16)
                return jnp.maximum(top, jnp.max(jnp.abs(hi).reshape(piece // 16, 16, columns), axis=0))

            top = lax.fori_loop(0, block // piece, convert, top)

            @pl.when(turn + slots < 2 * steps)
            def _():
                for copy in copies(turn + slots):
                    copy.start()

        inverse = ((TOP * 256.0) / jnp.full((1, 128), jnp.max(top.astype(F32)))).astype(BF16)
        unit = 1.0 / inverse.astype(F32)
        unit_ref[first + step] = unit
        high, rest = times_b(high_ref[k, 0, rows, :], high_ref[k, 1, rows, :], w_ref)
        high = high + rest
        for i in range(block // small):
            there = pl.ds(pl.multiple_of(at + i * small, small), small)
            for h in range(2):
                lo = rest_ref[h, i * small : i * small + small, :]
                low_ref[k, h, there, :] = (lo * inverse[:, :1]).astype(F8)
        low, rest = times_b(low_ref[k, 0, rows, :], low_ref[k, 1, rows, :], w8_ref)
        stored_ref[step // count, rows, :] = high + (low + rest * 0.0625) * (scale_ref[...] * unit)


def weights_kernel(bt_ref, w_ref, w8_ref, scale_ref):
    scale_ref[...] = second_weights(bt_ref, w_ref, w8_ref)


def pass_b_kernel(first, depth, high_ref, low_ref, unit_ref, w_ref, w8_ref, scale_ref, _, stored_ref):
    half = high_ref.shape[2]
    count = unit_ref.shape[0] // depth
    block = half // count
    chunk = min(CHUNK, half)

    for i in range(stored_ref.shape[0]):
        k = first + i
        for q in range(0, half, chunk):
            rows = slice(q, q + chunk)
            high, low = times_both(
                high_ref[k, 0, rows, :], high_ref[k, 1, rows, :],
                low_ref[k, 0, rows, :], low_ref[k, 1, rows, :], w_ref, w8_ref,
            )
            for at in range(0, chunk, block):
                here = slice(at, at + block)
                unit = unit_ref[k * count + (q + at) // block]
                stored_ref[i, q + at : q + at + block, :] = high[here] + low[here] * (scale_ref[...] * unit)


def pass_a_kernel(side, high_ref, low_ref, unit_ref, half_ref, other_ref, inv_ref, c_ref, *refs):
    p_out, sums_out, w_ref, w8_ref, a_ref = refs if side else refs[1:5] + refs[:1]
    depth, _, half, _ = high_ref.shape
    columns = p_out.shape[2]
    here = slice(side * columns, side * columns + columns)
    count = unit_ref.shape[0] // depth
    block = half // count
    part = half // 2
    core, _ = place()
    inv = inv_ref[...]
    a_ref[pl.ds(pl.multiple_of(core * part, part), part), :] = dot(half_ref[...], inv)
    a_ref[pl.ds(pl.multiple_of((1 - core) * part, part), part), :] = dot(other_ref[...], inv)
    at = a_ref[...].T
    if side == 0:
        gram = dot(at, at, ((1,), (1,)))
        sums_out[:, columns:] = wide(gram[:64, :64] + gram[64:, 64:])
    top = jnp.max(jnp.abs(at), axis=1, keepdims=True)
    unit = jnp.maximum(jnp.maximum(top[:64], top[64:]), TINY) / TOP
    for h in range(2):
        rows = at[64 * h : 64 * h + 64]
        hi, lo = split(rows)
        w_ref[h, :64, :] = hi
        w_ref[h, 64:, :] = lo
        hi8, lo8 = split8(rows, unit)
        w8_ref[h, :64, :] = hi8.astype(F8)
        w8_ref[h, 64:, :] = lo8.astype(F8)
    units = jnp.concatenate([unit, unit * 0.0625], axis=0)
    sums_out[:, :columns] = jnp.zeros((64, columns), F32)

    @pl.loop(0, depth)
    def _(k):
        row = jnp.sum(jnp.where(iota(depth, 128, 0) == k, c_ref[...], 0.0), axis=0, keepdims=True)
        col = col_of(row[:, :64])
        both = dot16(w_ref[0], high_ref[k, 0, :, here]) + dot16(w_ref[1], high_ref[k, 1, :, here])
        for b in range(count):
            rows = slice(b * block, b * block + block)
            low = dot16(w8_ref[0, :, rows], low_ref[k, 0, rows, here])
            low += dot16(w8_ref[1, :, rows], low_ref[k, 1, rows, here])
            both += (units * unit_ref[k * count + b][:, :1]) * low
        product = both[:64] + both[64:]
        p_out[k] = product
        sums_out[:, :columns] += col * product


def solve_b_kernel(share, a0_ref, a1_ref, b0_ref, b1_ref, gc_ref, p0_ref, p1_ref, bt_out, sums_out, ga_out, na_out, inv_ref):
    first, second = a0_ref[...] + a1_ref[...], b0_ref[...] + b1_ref[...]
    columns = second.shape[1]
    raw = first[:, columns : columns + 64]
    row, col = column_norms(raw)
    gram_a = raw / (row * col)
    invert_into(inv_ref, gram_a * gc_ref[...])
    bt = dot(inv_ref[...], jnp.concatenate([first[:, :columns], second], axis=1) / col)
    bt_out[...] = bt
    sums = wide(dot(bt, bt, ((1,), (1,)))) * share
    lane = iota(64, 128, 1)
    for k in range(p0_ref.shape[0]):
        three = jnp.sum(bt[:, :columns] * p0_ref[k] + bt[:, columns:] * p1_ref[k], axis=1, keepdims=True)
        sums = jnp.where(lane == 64 + k, three, sums)
    sums_out[...] = sums
    ga_out[...] = gram_a
    na_out[...] = row


def call(kernel, outs, *operands, scratch=(), mib=SMALL, name=None, flops=200000, nbytes=200000, first=VMEM, keep=(), written=()):
    going = [operands[i] for i in keep + written]
    results, held = len(outs), len(keep)

    def run(*refs):
        rest = refs[len(operands) :]
        kernel(*refs[: len(operands)], *rest[:results], *rest[results + held :])

    return pl.pallas_call(
        run,
        in_specs=[first] + [VMEM] * (len(operands) - 1),
        out_specs=[VMEM] * (results + len(going)),
        out_shape=outs + [pltpu.VMEM(x.shape, x.dtype) for x in going],
        scratch_shapes=scratch,
        input_output_aliases={i: results + n for n, i in enumerate(keep + written)},
        compiler_params=params(mib),
        cost_estimate=cost(flops, nbytes),
        name=name,
    )(*operands)


def resident(x):
    return pltpu.with_memory_space_constraint(x, pltpu.VMEM)


def add(*parts):
    return call(add_kernel, [shape(*parts[0].shape)], *parts, name="add")[0]


def inverse_space():
    return [pltpu.VMEM((64, 64), F32)]


def make_weights(bt):
    columns = bt.shape[1]
    return call(
        weights_kernel,
        [shape(2, columns, 128, dtype=BF16), shape(2, columns, 128, dtype=F8), shape(1, 128)],
        bt, name="weights",
    )


def load(tensor, bt, gram):
    depth, rows, columns = tensor.shape
    half = rows // 2
    block = min(256, half)
    weights, steps = list(make_weights(bt)), masks("ja")
    kept, stored = [], []
    for g in range(GROUPS):
        new = [] if kept else [
            pltpu.VMEM((depth, 2, half, columns), BF16),
            pltpu.VMEM((depth, 2, half, columns), F8),
            pltpu.VMEM((depth * (half // block), 1, 128), F32),
        ]
        outs = call(
            functools.partial(load_kernel, g),
            new + [pltpu.VMEM((depth // GROUPS, half, 128), F32)],
            tensor.reshape(depth, 2, half, columns), *weights, *[resident(x) for x in kept],
            first=pl.BlockSpec(memory_space=pl.ANY),
            scratch=[
                pltpu.VMEM((3, block, columns), F32), pltpu.VMEM((2, block, columns), BF16),
                pltpu.SemaphoreType.DMA((3, 2)),
            ],
            mib=SPACE, name="load", flops=6 * tensor.size * 64 // GROUPS, nbytes=4 * tensor.size // GROUPS,
            written=(4, 5, 6) if kept else (),
        )
        if kept:
            stored.append(outs[0])
            kept = outs[1:]
        else:
            kept, stored = outs[:3], [outs[3]]
        if len(steps) > 1:
            gram = add(gram, across(gram, *steps.pop(0)))
            weights[2], gram = lax.optimization_barrier((weights[2], gram))
    return kept, stored, butterfly(gram, steps)


def pass_a(kept, half, other, inv, c, side):
    depth, _, rows, columns = kept[0].shape
    columns //= 2
    *outs, high, low, unit = call(
        functools.partial(pass_a_kernel, side),
        ([] if side else [shape(rows, 128)])
        + [pltpu.VMEM((depth, 64, columns), F32), shape(64, columns if side else columns + 128)],
        *[resident(x) for x in kept], half, other, inv, c,
        scratch=[pltpu.VMEM((2, 128, rows), BF16), pltpu.VMEM((2, 128, rows), F8)]
        + [pltpu.VMEM((rows, 128), F32)] * side,
        mib=SPACE, name="pass_a", flops=3 * kept[0].size * 64, nbytes=3 * kept[0].size // 2, keep=(0, 1, 2),
    )
    return outs, [high, low, unit]


def pass_b(kept, stored, bt):
    weights = make_weights(bt)
    size = kept[0].size // GROUPS
    results = []
    for g, old in enumerate(stored):
        *kept, new = call(
            functools.partial(pass_b_kernel, g * old.shape[0], kept[0].shape[0]), [],
            *[resident(x) for x in kept], *weights, resident(old),
            mib=SPACE, name="pass_b", flops=6 * size * 64, nbytes=3 * size, keep=(0, 1, 2), written=(6,),
        )
        results.append(new)
    return kept, results


def across(x, axis, mask):
    n = lax.axis_size(axis)
    return lax.ppermute(x, axis, [(i, i ^ mask) for i in range(n)])


def masks(axis):
    return [(axis, 1 << b) for b in range(lax.axis_size(axis).bit_length() - 1)]


def butterfly(x, steps):
    for axis, mask in steps[:-1]:
        x = add(x, across(x, axis, mask))
    axis, mask = steps[-1]
    return x, across(x, axis, mask)


def body(tensor, b_init, c_init):
    depth, rows, columns = tensor.shape
    half = rows // 2
    n_ia, n_ja = lax.axis_size("ia"), lax.axis_size("ja")
    n_z = n_ja // 2
    ja = lax.axis_index("ja")
    piece = half // 2 // n_z

    everyone = masks("ja") + masks("ia")
    bt = b_init.T
    gram, c, gram_c = call(
        start_kernel, [shape(64, 128), shape(depth, 128), shape(64, 64)], bt, c_init, name="start",
    )
    kept, stored, grams = load(tensor, bt, gram)

    def sum_over_ja(keep, send, grams):
        recv = across(send, "ja", 1)
        if len(grams) == 2:
            (inv,) = call(inverse_kernel, [shape(128, 128)], *grams, scratch=inverse_space(), name="inverse")
            keep, inv = lax.optimization_barrier((keep, inv))
        own, *sends = call(
            spread_kernel, [shape(piece, 128)] * n_z, keep, recv, name="spread"
        )
        own = add(own, *[across(s, "ja", 2 * d) for d, s in enumerate(sends, 1)])
        parts = [own] + [across(own, "ja", 2 * d) for d in range(1, n_z)]
        (mine,) = call(gather_kernel, [shape(half // 2, 128)], *parts, name="gather")
        gram_b = None
        if len(grams) == 3:
            gram_b, inv = call(
                first_inverse_kernel, [shape(64, 64), shape(128, 128)], *grams,
                scratch=inverse_space(), name="inverse",
            )
        return mine, across(mine, "ja", 1), inv

    def sum_over_ia(first, second):
        order = masks("ia")
        return butterfly(first, order) + butterfly(second, order[1:] + order[:1])

    keep, send = call(
        contract_start_kernel, [shape(half // 2, 128)] * 2, c, *[resident(x) for x in stored],
        name="contract", flops=tensor.size // 8, nbytes=tensor.size // 4,
    )
    grams = grams + (gram_c,)
    for sweep in range(SWEEPS):
        last = sweep == SWEEPS - 1
        mine, other, inv = sum_over_ja(keep, send, grams)
        (a, left, first), kept = pass_a(kept, mine, other, inv, c, 0)
        (right, second), kept = pass_a(kept, mine, other, inv, c, 1)
        bt, sums, gram_a, norm_a = call(
            functools.partial(solve_b_kernel, 1.0 / n_ia),
            [shape(64, columns), shape(64, 128), shape(64, 64), shape(1, 64)],
            *sum_over_ia(first, second), gram_c, left, right, scratch=inverse_space(), mib=3, name="solve_b",
        )
        sums = butterfly(sums, everyone)
        if last:
            break
        kept, stored = pass_b(kept, stored, bt)
        c, gram_b, gram_c, keep, send = call(
            contract_kernel,
            [shape(depth, 128), shape(64, 64), shape(64, 64)] + [shape(half // 2, 128)] * 2,
            *sums, gram_a, norm_a, *[resident(x) for x in stored], scratch=inverse_space(),
            name="contract", flops=tensor.size // 8, nbytes=tensor.size // 4,
        )
        grams = (gram_b, gram_c)
    factor_c, bt, a = call(
        last_kernel, [shape(depth, 64), shape(64, columns), shape(half, 128)],
        *sums, gram_a, norm_a, bt, a, scratch=inverse_space(), mib=3, name="last",
    )
    share = rows // n_ja
    at = ja * share
    mine = lax.dynamic_slice_in_dim(a, at % half, share, 0)
    factor_a = jnp.where(at < half, mine[:, :64], mine[:, 64:])
    return factor_a, bt.T, factor_c


def solution(mesh):
    in_specs = (P(None, "ia", "ja"), P("ja", None), P())
    out_specs = (P(("ia", "ja"), None), P("ja", None), P())
    return jax.shard_map(body, mesh=mesh, in_specs=in_specs, out_specs=out_specs, check_vma=False)
```

```python
import functools

import jax
import jax.numpy as jnp
from jax import lax
from jax.experimental import pallas as pl
from jax.experimental.pallas import tpu as pltpu
from jax.sharding import PartitionSpec as P

SWEEPS = 4
EPS = 1e-6
HIGH = lax.Precision.HIGHEST
F32 = jnp.float32
BF16 = jnp.bfloat16
F8 = jnp.float8_e4m3fn
TOP = 224.0
TINY = 1e-30
GROUPS = 4
CHUNK = 1024
SLOTS = 3
SPACE = 6
SMALL = 1
VMEM = pl.BlockSpec(memory_space=pltpu.VMEM)
MIB = 1 << 20


def params(mib):
    return pltpu.CompilerParams(vmem_limit_bytes=int(mib * MIB))


def cost(flops, nbytes):
    return pl.CostEstimate(flops=int(flops), bytes_accessed=int(nbytes), transcendentals=0)


def shape(*dims, dtype=F32):
    return jax.ShapeDtypeStruct(dims, dtype)


def dot(a, b, dims=((1,), (0,))):
    return lax.dot_general(a, b, (dims, ((), ())), precision=HIGH, preferred_element_type=F32)


def dot16(a, b):
    return jnp.dot(a, b, preferred_element_type=F32)


def split(x):
    hi = x.astype(BF16)
    return hi, (x - hi.astype(F32)).astype(BF16)


def dot_parts(a, b):
    (a_hi, a_lo), (b_hi, b_lo) = split(a), split(b)
    return dot16(a_hi, b_hi) + (dot16(a_hi, b_lo) + dot16(a_lo, b_hi))


def times_t(a, b):
    return lax.dot_general(a, b, (((1,), (1,)), ((), ())), preferred_element_type=F32)


def iota(rows, cols, dim):
    return lax.broadcasted_iota(jnp.int32, (rows, cols), dim)


def eye(n):
    return (iota(n, n, 0) == iota(n, n, 1)).astype(F32)


def column_norms(raw):
    diagonal = raw * eye(raw.shape[0])
    row = jnp.sqrt(jnp.sum(diagonal, axis=0, keepdims=True) + EPS)
    col = jnp.sqrt(jnp.sum(diagonal, axis=1, keepdims=True) + EPS)
    return row, col


def eliminate(g):
    n = g.shape[0]
    m = jnp.concatenate([g, eye(n)], axis=1)
    rows = iota(n, 2 * n, 0)
    for k in range(n):
        pivot = m[k : k + 1, :] / m[k : k + 1, k : k + 1]
        m = jnp.where(rows == k, pivot, m - m[:, k : k + 1] * pivot)
    return m[:, n:]


def invert_into(out_ref, g):
    n = g.shape[0]
    one = eye(n)
    diagonal = g * one
    row = lax.rsqrt(jnp.sum(diagonal, axis=0, keepdims=True))
    col = lax.rsqrt(jnp.sum(diagonal, axis=1, keepdims=True))
    power = one - g * (row * col)
    close = jnp.sum(power * power) <= 0.25

    @pl.when(close)
    def _():
        e = power
        total = one + e
        for _ in range(4):
            e = dot(e, e)
            total = total + dot(total, e)
        out_ref[...] = total * (row * col)

    @pl.when(jnp.logical_not(close))
    def _():
        out_ref[...] = eliminate(g)


def block_diagonal(g):
    zero = jnp.zeros_like(g)
    return jnp.concatenate(
        [jnp.concatenate([g, zero], axis=1), jnp.concatenate([zero, g], axis=1)], axis=0
    )


def wide(x):
    return jnp.concatenate([x, x], axis=1)


def row_of(col):
    return jnp.sum(eye(col.shape[0]) * col, axis=0, keepdims=True)


def col_of(row):
    return jnp.sum(eye(row.shape[1]) * row, axis=1, keepdims=True)


def split8(x, unit):
    x = x / unit
    hi = x.astype(F8).astype(F32)
    return hi, ((x - hi) * 16.0).astype(F8).astype(F32)


def start_kernel(bt_ref, c_ref, gb_ref, c_out, gc_ref):
    bt = bt_ref[...]
    gb_ref[...] = wide(dot(bt, bt, ((1,), (1,))))
    c = c_ref[...]
    c_out[...] = wide(c)
    gc_ref[...] = dot(c, c, ((0,), (0,)))


def first_inverse_kernel(x_ref, y_ref, gc_ref, gb_out, inv_out, inv_ref):
    gram_b = x_ref[:, :64] + y_ref[:, :64]
    gb_out[...] = gram_b
    invert_into(inv_ref, gram_b * gc_ref[...])
    inv_out[...] = block_diagonal(inv_ref[...])


def inverse_kernel(x_ref, y_ref, out_ref, inv_ref):
    invert_into(inv_ref, x_ref[...] * y_ref[...])
    out_ref[...] = block_diagonal(inv_ref[...])


def third_factor(depth, x_ref, y_ref, ga_ref, na_ref, inv_ref):
    total = x_ref[...] + y_ref[...]
    raw = total[:, :64]
    row, col = column_norms(raw)
    gram_b = raw / (row * col)
    invert_into(inv_ref, gram_b * ga_ref[...])
    three = total.T[64 : 64 + depth, :] / (na_ref[...] * row)
    return dot(three, inv_ref[...]), gram_b, row, col


def last_kernel(x_ref, y_ref, ga_ref, na_ref, bt_ref, a_ref, c_out, b_out, a_out, inv_ref):
    c, _, _, col = third_factor(c_out.shape[0], x_ref, y_ref, ga_ref, na_ref, inv_ref)
    c_out[...] = c
    b_out[...] = bt_ref[...] / col
    a_out[...] = a_ref[...] / wide(na_ref[...])


def place():
    ja = lax.axis_index("ja")
    return lax.rem(ja, 2), lax.div(ja, 2)


def add_kernel(*refs):
    parts = [r[...] for r in refs[:-1]]
    while len(parts) > 1:
        parts = [parts[i] + parts[i + 1] for i in range(0, len(parts), 2)]
    refs[-1][...] = parts[0]


def contract(stored_refs, scaled, keep_ref, send_ref):
    depth = scaled.shape[0]
    group = depth // len(stored_refs)
    part = stored_refs[0].shape[1] // 2
    chunk = min(64, part)
    core, _ = place()
    for out, which in ((keep_ref, core), (send_ref, 1 - core)):

        @pl.loop(0, part // chunk)
        def _(i):
            at = pl.multiple_of(which * part + i * chunk, chunk)
            total = None
            for k in range(depth):
                term = stored_refs[k // group][k % group, pl.ds(at, chunk), :] * scaled[k : k + 1, :]
                total = term if total is None else total + term
            out[pl.ds(pl.multiple_of(i * chunk, chunk), chunk), :] = total


def contract_start_kernel(c_ref, *refs):
    contract(refs[:GROUPS], c_ref[...], *refs[GROUPS:])


def contract_kernel(x_ref, y_ref, ga_ref, na_ref, *refs):
    c_out, gb_out, gc_out, keep_ref, send_ref, inv_ref = refs[GROUPS:]
    c, gram_b, norm, _ = third_factor(c_out.shape[0], x_ref, y_ref, ga_ref, na_ref, inv_ref)
    c_out[...] = wide(c)
    gb_out[...] = gram_b
    gc_out[...] = dot(c, c, ((0,), (0,)))
    contract(refs[:GROUPS], wide(c / norm), keep_ref, send_ref)


def spread_kernel(keep_ref, recv_ref, own_ref, *send_refs):
    rows = own_ref.shape[0]
    _, z = place()
    for d, out in enumerate((own_ref,) + send_refs):
        at = pl.multiple_of((z ^ d) * rows, rows)
        out[...] = keep_ref[pl.ds(at, rows), :] + recv_ref[pl.ds(at, rows), :]


def gather_kernel(*refs):
    parts, out = refs[:-1], refs[-1]
    rows = parts[0].shape[0]
    _, z = place()
    for d, part in enumerate(parts):
        at = pl.multiple_of((z ^ d) * rows, rows)
        out[pl.ds(at, rows), :] = part[...]


def second_weights(bt_ref, w_ref, w8_ref):
    unit = jnp.maximum(jnp.max(jnp.abs(bt_ref[...]), axis=1, keepdims=True), TINY) / TOP
    columns = bt_ref.shape[1]
    chunk = min(128, columns)

    @pl.loop(0, columns // chunk)
    def _(i):
        here = pl.ds(pl.multiple_of(i * chunk, chunk), chunk)
        part = bt_ref[:, here]
        hi = part.astype(BF16).astype(F32)
        for out, parts in ((w_ref, (hi, part - hi)), (w8_ref, split8(part, unit))):
            b = jnp.concatenate(parts, axis=0).T
            turned = pltpu.roll(b, 64, 1)
            out[0, here, :] = b.astype(out.dtype)
            out[1, here, :] = turned.astype(out.dtype)

    return wide(row_of(unit))


def times_b(first, second, weights):
    x, y = dot16(first, weights[0]), dot16(second, weights[1])
    left = iota(*x.shape, 1) < 64
    return jnp.where(left, x, y), pltpu.roll(jnp.where(left, y, x), 64, 1)


def times_both(high0, high1, low0, low1, w_ref, w8_ref):
    high, high_rest = times_b(high0, high1, w_ref)
    low, low_rest = times_b(low0, low1, w8_ref)
    return high + high_rest, low + low_rest * 0.0625


def load_kernel(group, *refs):
    (t_ref, w_ref, w8_ref, scale_ref), refs = refs[:4], refs[4 if group == 0 else 7 :]
    high_ref, low_ref, unit_ref, stored_ref, ring, rest_ref, sems = refs if group == 0 else refs[1:4] + refs[:1] + refs[4:]
    size, half, _ = stored_ref.shape
    columns = t_ref.shape[3]
    slots, block, _ = ring.shape
    count = half // block
    first, steps = group * size * count, size * count
    piece, small, part = min(64, block), min(32, block), block // 2

    def copies(turn):
        step, h = turn // 2, turn % 2
        k, at = (first + step) // count, (step % count) * block
        return [
            pltpu.make_async_copy(
                t_ref.at[k, h, pl.ds(pl.multiple_of(at + p * part, part), part), :],
                ring.at[turn % slots, pl.ds(p * part, part), :],
                sems.at[turn % slots, p],
            )
            for p in range(2)
        ]

    for turn in range(slots):
        for copy in copies(turn):
            copy.start()

    @pl.loop(0, steps)
    def _(step):
        k, at = (first + step) // count, pl.multiple_of((step % count) * block, block)
        rows = pl.ds(at, block)
        top = jnp.full((16, columns), TINY, BF16)
        for h in range(2):
            turn = 2 * step + h
            for copy in copies(turn):
                copy.wait()

            def convert(i, top):
                here = pl.ds(pl.multiple_of(i * piece, piece), piece)
                there = pl.ds(pl.multiple_of(at + i * piece, piece), piece)
                t = ring[turn % slots, here, :]
                hi = t.astype(BF16)
                high_ref[k, h, there, :] = hi
                rest_ref[h, here, :] = (t - hi.astype(F32)).astype(BF16)
                return jnp.maximum(top, jnp.max(jnp.abs(hi).reshape(piece // 16, 16, columns), axis=0))

            top = lax.fori_loop(0, block // piece, convert, top)

            @pl.when(turn + slots < 2 * steps)
            def _():
                for copy in copies(turn + slots):
                    copy.start()

        inverse = ((TOP * 256.0) / jnp.full((1, 128), jnp.max(top.astype(F32)))).astype(BF16)
        unit = 1.0 / inverse.astype(F32)
        unit_ref[first + step] = unit
        high, rest = times_b(high_ref[k, 0, rows, :], high_ref[k, 1, rows, :], w_ref)
        high = high + rest
        for i in range(block // small):
            there = pl.ds(pl.multiple_of(at + i * small, small), small)
            for h in range(2):
                lo = rest_ref[h, i * small : i * small + small, :]
                low_ref[k, h, there, :] = (lo * inverse[:, :1]).astype(F8)
        low, rest = times_b(low_ref[k, 0, rows, :], low_ref[k, 1, rows, :], w8_ref)
        stored_ref[step // count, rows, :] = high + (low + rest * 0.0625) * (scale_ref[...] * unit)


def weights_kernel(bt_ref, w_ref, w8_ref, scale_ref):
    scale_ref[...] = second_weights(bt_ref, w_ref, w8_ref)


def pass_b_kernel(first, depth, high_ref, low_ref, unit_ref, w_ref, w8_ref, scale_ref, _, stored_ref):
    half = high_ref.shape[2]
    count = unit_ref.shape[0] // depth
    block = half // count
    chunk = min(CHUNK, half)

    for i in range(stored_ref.shape[0]):
        k = first + i
        for q in range(0, half, chunk):
            rows = slice(q, q + chunk)
            high, low = times_both(
                high_ref[k, 0, rows, :], high_ref[k, 1, rows, :],
                low_ref[k, 0, rows, :], low_ref[k, 1, rows, :], w_ref, w8_ref,
            )
            for at in range(0, chunk, block):
                here = slice(at, at + block)
                unit = unit_ref[k * count + (q + at) // block]
                stored_ref[i, q + at : q + at + block, :] = high[here] + low[here] * (scale_ref[...] * unit)


def pass_a_kernel(high_ref, low_ref, unit_ref, half_ref, other_ref, inv_ref, c_ref,
                  a_out, p_out, first_out, second_out, w_ref, w8_ref, acc_ref):
    depth, _, half, columns = high_ref.shape
    count = unit_ref.shape[0] // depth
    block = half // count
    part = half // 2
    core, _ = place()
    inv = inv_ref[...]
    a_out[pl.ds(pl.multiple_of(core * part, part), part), :] = dot_parts(half_ref[...], inv)
    a_out[pl.ds(pl.multiple_of((1 - core) * part, part), part), :] = dot_parts(other_ref[...], inv)
    at = a_out[...].T
    top = jnp.max(jnp.abs(at), axis=1, keepdims=True)
    unit = jnp.maximum(jnp.maximum(top[:64], top[64:]), TINY) / TOP
    for h in range(2):
        rows = at[64 * h : 64 * h + 64]
        hi, lo = split(rows)
        w_ref[h, :64, :] = hi
        w_ref[h, 64:, :] = lo
        hi8, lo8 = split8(rows, unit)
        w8_ref[h, :64, :] = hi8.astype(F8)
        w8_ref[h, 64:, :] = lo8.astype(F8)
    gram = times_t(w_ref[0], w_ref[0]) + times_t(w_ref[1], w_ref[1])
    gram = gram[:64] + gram[64:]
    gram = wide(gram[:, :64] + gram[:, 64:])
    units = jnp.concatenate([unit, unit * 0.0625], axis=0)
    acc_ref[...] = jnp.zeros_like(acc_ref)

    @pl.loop(0, depth)
    def _(k):
        row = jnp.sum(jnp.where(iota(depth, 128, 0) == k, c_ref[...], 0.0), axis=0, keepdims=True)
        col = col_of(row[:, :64])
        both = dot16(w_ref[0], high_ref[k, 0]) + dot16(w_ref[1], high_ref[k, 1])
        for b in range(count):
            rows = slice(b * block, b * block + block)
            low = dot16(w8_ref[0, :, rows], low_ref[k, 0, rows, :])
            low += dot16(w8_ref[1, :, rows], low_ref[k, 1, rows, :])
            both += (units * unit_ref[k * count + b][:, :1]) * low
        product = both[:64] + both[64:]
        p_out[k] = product
        acc_ref[...] += col * product

    total = acc_ref[...]
    first_out[:, :columns] = total[:32]
    second_out[:, :columns] = total[32:]
    first_out[:, columns:] = gram[:32]
    second_out[:, columns:] = gram[32:]


def solve_b_kernel(share, a0_ref, a1_ref, b0_ref, b1_ref, gc_ref, p_ref, bt_out, sums_out, ga_out, na_out, inv_ref):
    total = jnp.concatenate([a0_ref[...] + a1_ref[...], b0_ref[...] + b1_ref[...]], axis=0)
    columns = bt_out.shape[1]
    raw = total[:, columns : columns + 64]
    row, col = column_norms(raw)
    gram_a = raw / (row * col)
    invert_into(inv_ref, gram_a * gc_ref[...])
    bt = dot(inv_ref[...], total[:, :columns] / col)
    bt_out[...] = bt
    sums = wide(dot(bt, bt, ((1,), (1,)))) * share
    lane = iota(64, 128, 1)
    for k in range(p_ref.shape[0]):
        sums = jnp.where(lane == 64 + k, jnp.sum(bt * p_ref[k], axis=1, keepdims=True), sums)
    sums_out[...] = sums
    ga_out[...] = gram_a
    na_out[...] = row


def call(kernel, outs, *operands, scratch=(), mib=SMALL, name=None, flops=200000, nbytes=200000, first=VMEM, keep=(), written=()):
    going = [operands[i] for i in keep + written]
    results, held = len(outs), len(keep)

    def run(*refs):
        rest = refs[len(operands) :]
        kernel(*refs[: len(operands)], *rest[:results], *rest[results + held :])

    return pl.pallas_call(
        run,
        in_specs=[first] + [VMEM] * (len(operands) - 1),
        out_specs=[VMEM] * (results + len(going)),
        out_shape=outs + [pltpu.VMEM(x.shape, x.dtype) for x in going],
        scratch_shapes=scratch,
        input_output_aliases={i: results + n for n, i in enumerate(keep + written)},
        compiler_params=params(mib),
        cost_estimate=cost(flops, nbytes),
        name=name,
    )(*operands)


def resident(x):
    return pltpu.with_memory_space_constraint(x, pltpu.VMEM)


def add(*parts):
    return call(add_kernel, [shape(*parts[0].shape)], *parts, name="add")[0]


def inverse_space():
    return [pltpu.VMEM((64, 64), F32)]


def make_weights(bt, going=()):
    columns = bt.shape[1]
    dims = (2, columns, 128)
    outs = [pltpu.VMEM(dims, BF16), pltpu.VMEM(dims, F8)] if going else [shape(*dims, dtype=BF16), shape(*dims, dtype=F8)]
    w, w8, scale, *going = call(
        lambda bt_ref, *refs: weights_kernel(bt_ref, *refs[len(going) :]), outs + [shape(1, 128)],
        bt, *[resident(x) for x in going],
        mib=SPACE if going else SMALL, name="weights", keep=tuple(range(1, 1 + len(going))),
    )
    return [w, w8, scale], going


def load(tensor, bt, gram):
    depth, rows, columns = tensor.shape
    half = rows // 2
    block = min(256, half)
    weights, steps = make_weights(bt)[0], masks("ja")
    kept, stored = [], []
    for g in range(GROUPS):
        new = [] if kept else [
            pltpu.VMEM((depth, 2, half, columns), BF16),
            pltpu.VMEM((depth, 2, half, columns), F8),
            pltpu.VMEM((depth * (half // block), 1, 128), F32),
        ]
        outs = call(
            functools.partial(load_kernel, g),
            new + [pltpu.VMEM((depth // GROUPS, half, 128), F32)],
            tensor.reshape(depth, 2, half, columns), *weights, *[resident(x) for x in kept],
            first=pl.BlockSpec(memory_space=pl.ANY),
            scratch=[
                pltpu.VMEM((SLOTS, block, columns), F32), pltpu.VMEM((2, block, columns), BF16),
                pltpu.SemaphoreType.DMA((SLOTS, 2)),
            ],
            mib=SPACE, name="load", flops=6 * tensor.size * 64 // GROUPS, nbytes=4 * tensor.size // GROUPS,
            written=(4, 5, 6) if kept else (),
        )
        if kept:
            stored.append(outs[0])
            kept = outs[1:]
        else:
            kept, stored = outs[:3], [outs[3]]
        if len(steps) > 1:
            gram = add(gram, across(gram, *steps.pop(0)))
            weights[2], gram = lax.optimization_barrier((weights[2], gram))
    return kept, stored, butterfly(gram, steps)


def pass_a(kept, half, other, inv, c):
    depth, _, rows, columns = kept[0].shape
    *outs, high, low, unit = call(
        pass_a_kernel,
        [shape(rows, 128), pltpu.VMEM((depth, 64, columns), F32)] + [pltpu.VMEM((32, columns + 128), F32)] * 2,
        *[resident(x) for x in kept], half, other, inv, c,
        scratch=[
            pltpu.VMEM((2, 128, rows), BF16), pltpu.VMEM((2, 128, rows), F8),
            pltpu.VMEM((64, columns), F32),
        ],
        mib=SPACE, name="pass_a", flops=6 * kept[0].size * 64, nbytes=3 * kept[0].size, keep=(0, 1, 2),
    )
    return outs, [high, low, unit]


def pass_b(kept, stored, bt):
    weights, going = make_weights(bt, kept + stored)
    kept, stored = going[:3], going[3:]
    weights = [resident(weights[0]), resident(weights[1]), weights[2]]
    size = kept[0].size // GROUPS
    results = []
    for g, old in enumerate(stored):
        *kept, new = call(
            functools.partial(pass_b_kernel, g * old.shape[0], kept[0].shape[0]), [],
            *[resident(x) for x in kept], *weights, resident(old),
            mib=SPACE, name="pass_b", flops=6 * size * 64, nbytes=3 * size, keep=(0, 1, 2), written=(6,),
        )
        results.append(new)
    return kept, results


def across(x, axis, mask):
    n = lax.axis_size(axis)
    return lax.ppermute(x, axis, [(i, i ^ mask) for i in range(n)])


def masks(axis):
    return [(axis, 1 << b) for b in range(lax.axis_size(axis).bit_length() - 1)]


def butterfly(x, steps):
    for axis, mask in steps[:-1]:
        x = add(x, across(x, axis, mask))
    axis, mask = steps[-1]
    return x, across(x, axis, mask)


def body(tensor, b_init, c_init):
    depth, rows, columns = tensor.shape
    half = rows // 2
    n_ia, n_ja = lax.axis_size("ia"), lax.axis_size("ja")
    n_z = n_ja // 2
    ja = lax.axis_index("ja")
    piece = half // 2 // n_z

    everyone = masks("ja") + masks("ia")
    bt = b_init.T
    gram, c, gram_c = call(
        start_kernel, [shape(64, 128), shape(depth, 128), shape(64, 64)], bt, c_init, name="start",
    )
    kept, stored, grams = load(tensor, bt, gram)

    def sum_over_ja(keep, send, grams):
        recv = across(send, "ja", 1)
        if len(grams) == 2:
            (inv,) = call(inverse_kernel, [shape(128, 128)], *grams, scratch=inverse_space(), name="inverse")
            keep, inv = lax.optimization_barrier((keep, inv))
        own, *sends = call(
            spread_kernel, [shape(piece, 128)] * n_z, keep, recv, name="spread"
        )
        own = add(own, *[across(s, "ja", 2 * d) for d, s in enumerate(sends, 1)])
        parts = [own] + [across(own, "ja", 2 * d) for d in range(1, n_z)]
        (mine,) = call(gather_kernel, [shape(half // 2, 128)], *parts, name="gather")
        gram_b = None
        if len(grams) == 3:
            gram_b, inv = call(
                first_inverse_kernel, [shape(64, 64), shape(128, 128)], *grams,
                scratch=inverse_space(), name="inverse",
            )
        return mine, across(mine, "ja", 1), inv

    def sum_over_ia(first, second):
        order = masks("ia")
        return butterfly(first, order) + butterfly(second, order[1:] + order[:1])

    keep, send = call(
        contract_start_kernel, [shape(half // 2, 128)] * 2, c, *stored,
        name="contract", flops=tensor.size // 8, nbytes=tensor.size // 4,
    )
    grams = grams + (gram_c,)
    for sweep in range(SWEEPS):
        last = sweep == SWEEPS - 1
        mine, other, inv = sum_over_ja(keep, send, grams)
        (a, products, first, second), kept = pass_a(kept, mine, other, inv, c)
        bt, sums, gram_a, norm_a = call(
            functools.partial(solve_b_kernel, 1.0 / n_ia),
            [shape(64, columns), shape(64, 128), shape(64, 64), shape(1, 64)],
            *sum_over_ia(first, second), gram_c, products, scratch=inverse_space(), name="solve_b",
        )
        sums = butterfly(sums, everyone)
        if last:
            break
        kept, stored = pass_b(kept, stored, bt)
        c, gram_b, gram_c, keep, send = call(
            contract_kernel,
            [shape(depth, 128), shape(64, 64), shape(64, 64)] + [shape(half // 2, 128)] * 2,
            *sums, gram_a, norm_a, *stored, scratch=inverse_space(),
            name="contract", flops=tensor.size // 8, nbytes=tensor.size // 4,
        )
        grams = (gram_b, gram_c)
    factor_c, bt, a = call(
        last_kernel, [shape(depth, 64), shape(64, columns), shape(half, 128)],
        *sums, gram_a, norm_a, bt, a, scratch=inverse_space(), name="last",
    )
    share = rows // n_ja
    at = ja * share
    mine = lax.dynamic_slice_in_dim(a, at % half, share, 0)
    factor_a = jnp.where(at < half, mine[:, :64], mine[:, 64:])
    return factor_a, bt.T, factor_c


def solution(mesh):
    in_specs = (P(None, "ia", "ja"), P("ja", None), P())
    out_specs = (P(("ia", "ja"), None), P("ja", None), P())
    return jax.shard_map(body, mesh=mesh, in_specs=in_specs, out_specs=out_specs, check_vma=False)
```

```python
import functools

import jax
import jax.numpy as jnp
from jax import lax
from jax.experimental import pallas as pl
from jax.experimental.pallas import tpu as pltpu
from jax.sharding import PartitionSpec as P

SWEEPS = 4
EPS = 1e-6
HIGH = lax.Precision.HIGHEST
F32 = jnp.float32
BF16 = jnp.bfloat16
F8 = jnp.float8_e4m3fn
TOP = 224.0
TINY = 1e-30
GROUPS = 4
CHUNK = 1024
SLOTS = 3
SPACE = 6
SMALL = 1
VMEM = pl.BlockSpec(memory_space=pltpu.VMEM)
MIB = 1 << 20


def params(mib):
    return pltpu.CompilerParams(vmem_limit_bytes=int(mib * MIB))


def cost(flops, nbytes):
    return pl.CostEstimate(flops=int(flops), bytes_accessed=int(nbytes), transcendentals=0)


def shape(*dims, dtype=F32):
    return jax.ShapeDtypeStruct(dims, dtype)


def dot(a, b, dims=((1,), (0,))):
    return lax.dot_general(a, b, (dims, ((), ())), precision=HIGH, preferred_element_type=F32)


def dot16(a, b):
    return jnp.dot(a, b, preferred_element_type=F32)


def split(x):
    hi = x.astype(BF16)
    return hi, (x - hi.astype(F32)).astype(BF16)


def dot_parts(a, b):
    (a_hi, a_lo), (b_hi, b_lo) = split(a), split(b)
    return dot16(a_hi, b_hi) + (dot16(a_hi, b_lo) + dot16(a_lo, b_hi))


def times_t(a, b):
    return lax.dot_general(a, b, (((1,), (1,)), ((), ())), preferred_element_type=F32)


def iota(rows, cols, dim):
    return lax.broadcasted_iota(jnp.int32, (rows, cols), dim)


def eye(n):
    return (iota(n, n, 0) == iota(n, n, 1)).astype(F32)


def column_norms(raw):
    diagonal = raw * eye(raw.shape[0])
    row = jnp.sqrt(jnp.sum(diagonal, axis=0, keepdims=True) + EPS)
    col = jnp.sqrt(jnp.sum(diagonal, axis=1, keepdims=True) + EPS)
    return row, col


def eliminate(g):
    n = g.shape[0]
    m = jnp.concatenate([g, eye(n)], axis=1)
    rows = iota(n, 2 * n, 0)
    for k in range(n):
        pivot = m[k : k + 1, :] / m[k : k + 1, k : k + 1]
        m = jnp.where(rows == k, pivot, m - m[:, k : k + 1] * pivot)
    return m[:, n:]


def invert_into(out_ref, g):
    n = g.shape[0]
    one = eye(n)
    diagonal = g * one
    row = lax.rsqrt(jnp.sum(diagonal, axis=0, keepdims=True))
    col = lax.rsqrt(jnp.sum(diagonal, axis=1, keepdims=True))
    power = one - g * (row * col)
    close = jnp.sum(power * power) <= 0.25

    @pl.when(close)
    def _():
        e = power
        total = one + e
        for _ in range(4):
            e = dot_parts(e, e)
            total = total + dot_parts(total, e)
        out_ref[...] = total * (row * col)

    @pl.when(jnp.logical_not(close))
    def _():
        out_ref[...] = eliminate(g)


def block_diagonal(g):
    zero = jnp.zeros_like(g)
    return jnp.concatenate(
        [jnp.concatenate([g, zero], axis=1), jnp.concatenate([zero, g], axis=1)], axis=0
    )


def wide(x):
    return jnp.concatenate([x, x], axis=1)


def row_of(col):
    return jnp.sum(eye(col.shape[0]) * col, axis=0, keepdims=True)


def col_of(row):
    return jnp.sum(eye(row.shape[1]) * row, axis=1, keepdims=True)


def split8(x, unit):
    x = x / unit
    hi = x.astype(F8).astype(F32)
    return hi, ((x - hi) * 16.0).astype(F8).astype(F32)


def start_kernel(bt_ref, c_ref, gb_ref, c_out, gc_ref):
    bt = bt_ref[...]
    gb_ref[...] = wide(dot(bt, bt, ((1,), (1,))))
    c = c_ref[...]
    c_out[...] = wide(c)
    gc_ref[...] = dot(c, c, ((0,), (0,)))


def first_inverse_kernel(x_ref, y_ref, gc_ref, gb_out, inv_out, inv_ref):
    gram_b = x_ref[:, :64] + y_ref[:, :64]
    gb_out[...] = gram_b
    invert_into(inv_ref, gram_b * gc_ref[...])
    inv_out[...] = block_diagonal(inv_ref[...])


def inverse_kernel(x_ref, y_ref, out_ref, inv_ref):
    invert_into(inv_ref, x_ref[...] * y_ref[...])
    out_ref[...] = block_diagonal(inv_ref[...])


def third_factor(depth, x_ref, y_ref, ga_ref, na_ref, inv_ref):
    total = x_ref[...] + y_ref[...]
    raw = total[:, :64]
    row, col = column_norms(raw)
    gram_b = raw / (row * col)
    invert_into(inv_ref, gram_b * ga_ref[...])
    three = total.T[64 : 64 + depth, :] / (na_ref[...] * row)
    return dot(three, inv_ref[...]), gram_b, row, col


def last_kernel(x_ref, y_ref, ga_ref, na_ref, bt_ref, a_ref, c_out, b_out, a_out, inv_ref):
    c, _, _, col = third_factor(c_out.shape[0], x_ref, y_ref, ga_ref, na_ref, inv_ref)
    c_out[...] = c
    b_out[...] = bt_ref[...] / col
    a_out[...] = a_ref[...] / wide(na_ref[...])


def place():
    ja = lax.axis_index("ja")
    return lax.rem(ja, 2), lax.div(ja, 2)


def add_kernel(*refs):
    parts = [r[...] for r in refs[:-1]]
    while len(parts) > 1:
        parts = [parts[i] + parts[i + 1] for i in range(0, len(parts), 2)]
    refs[-1][...] = parts[0]


def contract(stored_refs, scaled, keep_ref, send_ref):
    depth = scaled.shape[0]
    group = depth // len(stored_refs)
    part = stored_refs[0].shape[1] // 2
    chunk = min(64, part)
    core, _ = place()
    for out, which in ((keep_ref, core), (send_ref, 1 - core)):

        @pl.loop(0, part // chunk)
        def _(i):
            at = pl.multiple_of(which * part + i * chunk, chunk)
            total = None
            for k in range(depth):
                term = stored_refs[k // group][k % group, pl.ds(at, chunk), :] * scaled[k : k + 1, :]
                total = term if total is None else total + term
            out[pl.ds(pl.multiple_of(i * chunk, chunk), chunk), :] = total


def contract_start_kernel(c_ref, *refs):
    contract(refs[:GROUPS], c_ref[...], *refs[GROUPS:])


def contract_kernel(x_ref, y_ref, ga_ref, na_ref, *refs):
    c_out, gb_out, gc_out, keep_ref, send_ref, inv_ref = refs[GROUPS:]
    c, gram_b, norm, _ = third_factor(c_out.shape[0], x_ref, y_ref, ga_ref, na_ref, inv_ref)
    c_out[...] = wide(c)
    gb_out[...] = gram_b
    gc_out[...] = dot(c, c, ((0,), (0,)))
    contract(refs[:GROUPS], wide(c / norm), keep_ref, send_ref)


def spread_kernel(keep_ref, recv_ref, own_ref, *send_refs):
    rows = own_ref.shape[0]
    _, z = place()
    for d, out in enumerate((own_ref,) + send_refs):
        at = pl.multiple_of((z ^ d) * rows, rows)
        out[...] = keep_ref[pl.ds(at, rows), :] + recv_ref[pl.ds(at, rows), :]


def gather_kernel(*refs):
    parts, out = refs[:-1], refs[-1]
    rows = parts[0].shape[0]
    _, z = place()
    for d, part in enumerate(parts):
        at = pl.multiple_of((z ^ d) * rows, rows)
        out[pl.ds(at, rows), :] = part[...]


def second_weights(bt_ref, w_ref, w8_ref):
    unit = jnp.maximum(jnp.max(jnp.abs(bt_ref[...]), axis=1, keepdims=True), TINY) / TOP
    columns = bt_ref.shape[1]
    chunk = min(128, columns)

    @pl.loop(0, columns // chunk)
    def _(i):
        here = pl.ds(pl.multiple_of(i * chunk, chunk), chunk)
        part = bt_ref[:, here]
        hi = part.astype(BF16).astype(F32)
        for out, parts in ((w_ref, (hi, part - hi)), (w8_ref, split8(part, unit))):
            b = jnp.concatenate(parts, axis=0).T
            turned = pltpu.roll(b, 64, 1)
            out[0, here, :] = b.astype(out.dtype)
            out[1, here, :] = turned.astype(out.dtype)

    return wide(row_of(unit))


def times_b(first, second, weights):
    return side_by_side(dot16(first, weights[0]), dot16(second, weights[1]))


def side_by_side(x, y):
    left = iota(*x.shape, 1) < 64
    return jnp.where(left, x, y), pltpu.roll(jnp.where(left, y, x), 64, 1)


def times_both(high0, high1, low0, low1, w_ref, w8_ref):
    high, high_rest = times_b(high0, high1, w_ref)
    low, low_rest = times_b(low0, low1, w8_ref)
    return high + high_rest, low + low_rest * 0.0625


def load_kernel(group, *refs):
    (t_ref, w_ref, w8_ref, scale_ref), refs = refs[:4], refs[4 if group == 0 else 7 :]
    high_ref, low_ref, unit_ref, stored_ref, ring, rest_ref, sems = refs if group == 0 else refs[1:4] + refs[:1] + refs[4:]
    size, half, _ = stored_ref.shape
    columns = t_ref.shape[3]
    slots, block, _ = ring.shape
    count = half // block
    first, steps = group * size * count, size * count
    piece, small, part = min(64, block), min(32, block), block // 2

    def copies(turn):
        step, h = turn // 2, turn % 2
        k, at = (first + step) // count, (step % count) * block
        return [
            pltpu.make_async_copy(
                t_ref.at[k, h, pl.ds(pl.multiple_of(at + p * part, part), part), :],
                ring.at[turn % slots, pl.ds(p * part, part), :],
                sems.at[turn % slots, p],
            )
            for p in range(2)
        ]

    for turn in range(slots):
        for copy in copies(turn):
            copy.start()

    @pl.loop(0, steps)
    def _(step):
        k, at = (first + step) // count, pl.multiple_of((step % count) * block, block)
        rows = pl.ds(at, block)
        def convert(turn, h, i, top):
            here = pl.ds(pl.multiple_of(i * piece, piece), piece)
            there = pl.ds(pl.multiple_of(at + i * piece, piece), piece)
            t = ring[turn % slots, here, :]
            hi = t.astype(BF16)
            high_ref[k, h, there, :] = hi
            rest_ref[h, here, :] = (t - hi.astype(F32)).astype(BF16)
            return jnp.maximum(top, jnp.max(jnp.abs(hi).reshape(piece // 16, 16, columns), axis=0))

        def follow(turn):
            @pl.when(turn + slots < 2 * steps)
            def _():
                for copy in copies(turn + slots):
                    copy.start()

        turn = 2 * step
        for copy in copies(turn):
            copy.wait()
        top = lax.fori_loop(
            0, block // piece, functools.partial(convert, turn, 0), jnp.full((16, columns), TINY, BF16)
        )
        follow(turn)
        for copy in copies(turn + 1):
            copy.wait()
        x = dot16(high_ref[k, 0, rows, :], w_ref[0])
        for i in range(block // piece):
            top = convert(turn + 1, 1, i, top)
        follow(turn + 1)
        inverse = ((TOP * 256.0) / jnp.full((1, 128), jnp.max(top.astype(F32)))).astype(BF16)
        unit = 1.0 / inverse.astype(F32)
        unit_ref[first + step] = unit
        high, rest = side_by_side(x, dot16(high_ref[k, 1, rows, :], w_ref[1]))
        high = high + rest
        for i in range(block // small):
            there = pl.ds(pl.multiple_of(at + i * small, small), small)
            for h in range(2):
                lo = rest_ref[h, i * small : i * small + small, :]
                low_ref[k, h, there, :] = (lo * inverse[:, :1]).astype(F8)
        low, rest = times_b(low_ref[k, 0, rows, :], low_ref[k, 1, rows, :], w8_ref)
        stored_ref[step // count, rows, :] = high + (low + rest * 0.0625) * (scale_ref[...] * unit)


def weights_kernel(bt_ref, w_ref, w8_ref, scale_ref):
    scale_ref[...] = second_weights(bt_ref, w_ref, w8_ref)


def pass_b_kernel(first, depth, high_ref, low_ref, unit_ref, w_ref, w8_ref, scale_ref, _, stored_ref):
    half = high_ref.shape[2]
    count = unit_ref.shape[0] // depth
    block = half // count
    chunk = min(CHUNK, half)

    for i in range(stored_ref.shape[0]):
        k = first + i
        for q in range(0, half, chunk):
            rows = slice(q, q + chunk)
            high, low = times_both(
                high_ref[k, 0, rows, :], high_ref[k, 1, rows, :],
                low_ref[k, 0, rows, :], low_ref[k, 1, rows, :], w_ref, w8_ref,
            )
            for at in range(0, chunk, block):
                here = slice(at, at + block)
                unit = unit_ref[k * count + (q + at) // block]
                stored_ref[i, q + at : q + at + block, :] = high[here] + low[here] * (scale_ref[...] * unit)


def pass_a_kernel(high_ref, low_ref, unit_ref, half_ref, other_ref, inv_ref, c_ref,
                  a_out, p_out, first_out, second_out, w_ref, w8_ref, acc_ref):
    depth, _, half, columns = high_ref.shape
    count = unit_ref.shape[0] // depth
    block = half // count
    part = half // 2
    core, _ = place()
    inv = inv_ref[...]
    a_out[pl.ds(pl.multiple_of(core * part, part), part), :] = dot_parts(half_ref[...], inv)
    a_out[pl.ds(pl.multiple_of((1 - core) * part, part), part), :] = dot_parts(other_ref[...], inv)
    at = a_out[...].T
    top = jnp.max(jnp.abs(at), axis=1, keepdims=True)
    unit = jnp.maximum(jnp.maximum(top[:64], top[64:]), TINY) / TOP
    for h in range(2):
        rows = at[64 * h : 64 * h + 64]
        hi, lo = split(rows)
        w_ref[h, :64, :] = hi
        w_ref[h, 64:, :] = lo
        hi8, lo8 = split8(rows, unit)
        w8_ref[h, :64, :] = hi8.astype(F8)
        w8_ref[h, 64:, :] = lo8.astype(F8)
    gram = times_t(w_ref[0], w_ref[0]) + times_t(w_ref[1], w_ref[1])
    gram = gram[:64] + gram[64:]
    gram = wide(gram[:, :64] + gram[:, 64:])
    units = jnp.concatenate([unit, unit * 0.0625], axis=0)
    acc_ref[...] = jnp.zeros_like(acc_ref)

    @pl.loop(0, depth)
    def _(k):
        row = jnp.sum(jnp.where(iota(depth, 128, 0) == k, c_ref[...], 0.0), axis=0, keepdims=True)
        col = col_of(row[:, :64])
        both = dot16(w_ref[0], high_ref[k, 0]) + dot16(w_ref[1], high_ref[k, 1])
        for b in range(count):
            rows = slice(b * block, b * block + block)
            low = dot16(w8_ref[0, :, rows], low_ref[k, 0, rows, :])
            low += dot16(w8_ref[1, :, rows], low_ref[k, 1, rows, :])
            both += (units * unit_ref[k * count + b][:, :1]) * low
        product = both[:64] + both[64:]
        p_out[k] = product
        acc_ref[...] += col * product

    total = acc_ref[...]
    first_out[:, :columns] = total[:32]
    second_out[:, :columns] = total[32:]
    first_out[:, columns:] = gram[:32]
    second_out[:, columns:] = gram[32:]


def solve_b_kernel(share, a0_ref, a1_ref, b0_ref, b1_ref, gc_ref, p_ref, bt_out, sums_out, ga_out, na_out, inv_ref):
    total = jnp.concatenate([a0_ref[...] + a1_ref[...], b0_ref[...] + b1_ref[...]], axis=0)
    columns = bt_out.shape[1]
    raw = total[:, columns : columns + 64]
    row, col = column_norms(raw)
    gram_a = raw / (row * col)
    invert_into(inv_ref, gram_a * gc_ref[...])
    bt = dot(inv_ref[...], total[:, :columns] / col)
    bt_out[...] = bt
    sums = wide(dot(bt, bt, ((1,), (1,)))) * share
    lane = iota(64, 128, 1)
    for k in range(p_ref.shape[0]):
        sums = jnp.where(lane == 64 + k, jnp.sum(bt * p_ref[k], axis=1, keepdims=True), sums)
    sums_out[...] = sums
    ga_out[...] = gram_a
    na_out[...] = row


def call(kernel, outs, *operands, scratch=(), mib=SMALL, name=None, flops=200000, nbytes=200000, first=VMEM, keep=(), written=()):
    going = [operands[i] for i in keep + written]
    results, held = len(outs), len(keep)

    def run(*refs):
        rest = refs[len(operands) :]
        kernel(*refs[: len(operands)], *rest[:results], *rest[results + held :])

    return pl.pallas_call(
        run,
        in_specs=[first] + [VMEM] * (len(operands) - 1),
        out_specs=[VMEM] * (results + len(going)),
        out_shape=outs + [pltpu.VMEM(x.shape, x.dtype) for x in going],
        scratch_shapes=scratch,
        input_output_aliases={i: results + n for n, i in enumerate(keep + written)},
        compiler_params=params(mib),
        cost_estimate=cost(flops, nbytes),
        name=name,
    )(*operands)


def resident(x):
    return pltpu.with_memory_space_constraint(x, pltpu.VMEM)


def add(*parts):
    return call(add_kernel, [shape(*parts[0].shape)], *parts, name="add")[0]


def inverse_space():
    return [pltpu.VMEM((64, 64), F32)]


def make_weights(bt, going=()):
    columns = bt.shape[1]
    dims = (2, columns, 128)
    outs = [pltpu.VMEM(dims, BF16), pltpu.VMEM(dims, F8)] if going else [shape(*dims, dtype=BF16), shape(*dims, dtype=F8)]
    w, w8, scale, *going = call(
        lambda bt_ref, *refs: weights_kernel(bt_ref, *refs[len(going) :]), outs + [shape(1, 128)],
        bt, *[resident(x) for x in going],
        mib=SPACE if going else SMALL, name="weights", keep=tuple(range(1, 1 + len(going))),
    )
    return [w, w8, scale], going


def load(tensor, bt, gram):
    depth, rows, columns = tensor.shape
    half = rows // 2
    block = min(256, half)
    weights, steps = make_weights(bt)[0], masks("ja")
    kept, stored = [], []
    for g in range(GROUPS):
        new = [] if kept else [
            pltpu.VMEM((depth, 2, half, columns), BF16),
            pltpu.VMEM((depth, 2, half, columns), F8),
            pltpu.VMEM((depth * (half // block), 1, 128), F32),
        ]
        outs = call(
            functools.partial(load_kernel, g),
            new + [pltpu.VMEM((depth // GROUPS, half, 128), F32)],
            tensor.reshape(depth, 2, half, columns), *weights, *[resident(x) for x in kept],
            first=pl.BlockSpec(memory_space=pl.ANY),
            scratch=[
                pltpu.VMEM((SLOTS, block, columns), F32), pltpu.VMEM((2, block, columns), BF16),
                pltpu.SemaphoreType.DMA((SLOTS, 2)),
            ],
            mib=SPACE, name="load", flops=6 * tensor.size * 64 // GROUPS, nbytes=4 * tensor.size // GROUPS,
            written=(4, 5, 6) if kept else (),
        )
        if kept:
            stored.append(outs[0])
            kept = outs[1:]
        else:
            kept, stored = outs[:3], [outs[3]]
        if len(steps) > 1:
            gram = add(gram, across(gram, *steps.pop(0)))
            weights[2], gram = lax.optimization_barrier((weights[2], gram))
    return kept, stored, butterfly(gram, steps)


def pass_a(kept, half, other, inv, c):
    depth, _, rows, columns = kept[0].shape
    *outs, high, low, unit = call(
        pass_a_kernel,
        [shape(rows, 128), pltpu.VMEM((depth, 64, columns), F32)] + [pltpu.VMEM((32, columns + 128), F32)] * 2,
        *[resident(x) for x in kept], half, other, inv, c,
        scratch=[
            pltpu.VMEM((2, 128, rows), BF16), pltpu.VMEM((2, 128, rows), F8),
            pltpu.VMEM((64, columns), F32),
        ],
        mib=SPACE, name="pass_a", flops=6 * kept[0].size * 64, nbytes=3 * kept[0].size, keep=(0, 1, 2),
    )
    return outs, [high, low, unit]


def pass_b(kept, stored, bt):
    weights, going = make_weights(bt, kept + stored)
    kept, stored = going[:3], going[3:]
    weights = [resident(weights[0]), resident(weights[1]), weights[2]]
    size = kept[0].size // GROUPS
    results = []
    for g, old in enumerate(stored):
        *kept, new = call(
            functools.partial(pass_b_kernel, g * old.shape[0], kept[0].shape[0]), [],
            *[resident(x) for x in kept], *weights, resident(old),
            mib=SPACE, name="pass_b", flops=6 * size * 64, nbytes=3 * size, keep=(0, 1, 2), written=(6,),
        )
        results.append(new)
    return kept, results


def across(x, axis, mask):
    n = lax.axis_size(axis)
    return lax.ppermute(x, axis, [(i, i ^ mask) for i in range(n)])


def masks(axis):
    return [(axis, 1 << b) for b in range(lax.axis_size(axis).bit_length() - 1)]


def butterfly(x, steps):
    for axis, mask in steps[:-1]:
        x = add(x, across(x, axis, mask))
    axis, mask = steps[-1]
    return x, across(x, axis, mask)


def body(tensor, b_init, c_init):
    depth, rows, columns = tensor.shape
    half = rows // 2
    n_ia, n_ja = lax.axis_size("ia"), lax.axis_size("ja")
    n_z = n_ja // 2
    ja = lax.axis_index("ja")
    piece = half // 2 // n_z

    everyone = masks("ja") + masks("ia")
    bt = b_init.T
    gram, c, gram_c = call(
        start_kernel, [shape(64, 128), shape(depth, 128), shape(64, 64)], bt, c_init, name="start",
    )
    kept, stored, grams = load(tensor, bt, gram)

    def sum_over_ja(keep, send, grams):
        recv = across(send, "ja", 1)
        if len(grams) == 2:
            (inv,) = call(inverse_kernel, [shape(128, 128)], *grams, scratch=inverse_space(), name="inverse")
            keep, inv = lax.optimization_barrier((keep, inv))
        own, *sends = call(
            spread_kernel, [shape(piece, 128)] * n_z, keep, recv, name="spread"
        )
        own = add(own, *[across(s, "ja", 2 * d) for d, s in enumerate(sends, 1)])
        parts = [own] + [across(own, "ja", 2 * d) for d in range(1, n_z)]
        (mine,) = call(gather_kernel, [shape(half // 2, 128)], *parts, name="gather")
        gram_b = None
        if len(grams) == 3:
            gram_b, inv = call(
                first_inverse_kernel, [shape(64, 64), shape(128, 128)], *grams,
                scratch=inverse_space(), name="inverse",
            )
        return mine, across(mine, "ja", 1), inv

    def sum_over_ia(first, second):
        order = masks("ia")
        return butterfly(first, order) + butterfly(second, order[1:] + order[:1])

    keep, send = call(
        contract_start_kernel, [shape(half // 2, 128)] * 2, c, *stored,
        name="contract", flops=tensor.size // 8, nbytes=tensor.size // 4,
    )
    grams = grams + (gram_c,)
    for sweep in range(SWEEPS):
        last = sweep == SWEEPS - 1
        mine, other, inv = sum_over_ja(keep, send, grams)
        (a, products, first, second), kept = pass_a(kept, mine, other, inv, c)
        bt, sums, gram_a, norm_a = call(
            functools.partial(solve_b_kernel, 1.0 / n_ia),
            [shape(64, columns), shape(64, 128), shape(64, 64), shape(1, 64)],
            *sum_over_ia(first, second), gram_c, products, scratch=inverse_space(), name="solve_b",
        )
        sums = butterfly(sums, everyone)
        if last:
            break
        kept, stored = pass_b(kept, stored, bt)
        c, gram_b, gram_c, keep, send = call(
            contract_kernel,
            [shape(depth, 128), shape(64, 64), shape(64, 64)] + [shape(half // 2, 128)] * 2,
            *sums, gram_a, norm_a, *stored, scratch=inverse_space(),
            name="contract", flops=tensor.size // 8, nbytes=tensor.size // 4,
        )
        grams = (gram_b, gram_c)
    factor_c, bt, a = call(
        last_kernel, [shape(depth, 64), shape(64, columns), shape(half, 128)],
        *sums, gram_a, norm_a, bt, a, scratch=inverse_space(), name="last",
    )
    share = rows // n_ja
    at = ja * share
    mine = lax.dynamic_slice_in_dim(a, at % half, share, 0)
    factor_a = jnp.where(at < half, mine[:, :64], mine[:, 64:])
    return factor_a, bt.T, factor_c


def solution(mesh):
    in_specs = (P(None, "ia", "ja"), P("ja", None), P())
    out_specs = (P(("ia", "ja"), None), P("ja", None), P())
    return jax.shard_map(body, mesh=mesh, in_specs=in_specs, out_specs=out_specs, check_vma=False)
```
